32 devices in a mesh: groups: 2 (over y), xz: 4 (over z), gy: 4 (over x, core).
Axes of the slice: x: 2, y: 2, z: 4, core: 2. Of those that a mesh axis runs over, the one named last changes fastest.
Arguments:
- vorticity: float32 [3, 64, 256, 256], P(None, ('groups', 'xz'), 'gy'), parts along dimension 1, may hold values from -6 to 6
- velocity: float32 [3, 64, 256, 256], P(None, ('groups', 'xz'), 'gy'), parts along dimension 1, may hold values from -4 to 4
- sources: bfloat16 [8, 3, 256, 256], P(('groups', 'xz'), None, 'gy'), parts along dimension 0, may hold values from -6 to 6
- incidence: int32 [8, 32, 2], P('groups'), parts along dimension 0, may hold values from 0 to 4
- azimuth: int32 [6], P('groups'), parts along dimension 0, may hold values from 0 to 3
Outputs:
- vorticity_out: float32 [3, 64, 256, 256], P(None, ('groups', 'xz'), 'gy'), parts along dimension 1
The draws below stay inside these ranges and needn't reach their ends.
There are 2 independent parts, one for each index of `groups`. The reference program is written for one: setup_inputs(seed, part) draws one part's arguments, and reference() takes and returns one part's arrays. A program takes and returns all parts, laid end to end along the dimension named above; each array names one. Nothing has to cross between parts.
Inputs may be any that keep to these rules, and one draw needn't show every extreme that they name: `incidence`: an entry below 4 names a source block; 4 marks an empty slot. `azimuth`: which row of incidence each step uses.
All inputs are finite; a program needn't handle non-finite values.
Results may differ from the reference program's by a relative error of at most 0.0003.
Values may be sent and summed in bfloat16 or wider, within the bound.
No kernel may reach another device: no remote copies, remote signals or barrier semaphores. Data moves between devices by JAX's collectives and lax.ppermute only.
A program may use at most 128 MiB of HBM per device.

```python
import jax
import jax.numpy as jnp

STEPS = 3
KS = 2
NAZ = 4
NSRC = 4
NX = 32
NY = 256
NZ = 256


def place_ends(values, own_key, least, largest):
    spot = [jax.random.randint(jax.random.fold_in(own_key, axis), (), 0, length) for axis, length in enumerate(values.shape)]
    longest = values.shape.index(max(values.shape))
    beside = spot[:longest] + [(spot[longest] + 1) % values.shape[longest]] + spot[longest + 1:]
    return values.at[tuple(spot)].set(least).at[tuple(beside)].set(largest)


def block_levels(key, dims, cuts, smallest, high):
    def one(position, parts):
        heights = jax.random.uniform(jax.random.fold_in(jax.random.fold_in(key, 6), position), (parts,), jnp.float32, smallest / len(cuts), high / len(cuts))
        return jnp.repeat(jnp.exp(heights), dims[position] // parts).reshape((-1,) + (1,) * (len(dims) - position - 1))

    factor_of = one(*cuts[0])
    for cut in cuts[1:]:
        factor_of = factor_of * one(*cut)
    return factor_of


def noise(own_key, dims, deviation, bound, cuts=(), kind=jnp.bfloat16):
    array = deviation * jax.random.normal(own_key, dims, jnp.float32)
    if cuts:
        array = array * block_levels(own_key, dims, cuts, -0.22, 0.18)
    return jnp.clip(array, -bound, bound).astype(kind)


def setup_inputs(seed: int = 0, part: int = 0) -> dict:
    arg_keys = jax.random.split(jax.random.key(seed), 6)
    part_splits = jax.random.split(jax.random.fold_in(arg_keys[5], part), 6)
    vorticity = noise(part_splits[0], (3, NX, NY, NZ), 1.0, 6.0, ((1, 4), (2, 4)), jnp.float32)
    velocity = noise(part_splits[1], (3, NX, NY, NZ), 1.0, 4.0, ((1, 4), (2, 4)), jnp.float32)
    sources = noise(part_splits[2], (NSRC, 3, NY, NZ), 1.0, 6.0, ((0, 4), (2, 4)))
    incidence = place_ends(jax.random.randint(part_splits[3], (NAZ, NX, KS), 0, NSRC + 1), jax.random.fold_in(part_splits[3], 1), 0, NSRC).astype(jnp.int32)
    azimuth = jax.random.randint(part_splits[4], (STEPS,), 0, NAZ).astype(jnp.int32)
    return dict(vorticity=vorticity, velocity=velocity, sources=sources, incidence=incidence, azimuth=azimuth)


time_step = 0.2
viscous = 0.1


def derivatives(padded):
    zpadded = jnp.pad(padded, ((0, 0), (0, 0), (0, 0), (1, 1)))
    center = zpadded[:, 1:-1, 1:-1, 1:-1]
    plus_x = zpadded[:, 2:, 1:-1, 1:-1]
    minus_x = zpadded[:, :-2, 1:-1, 1:-1]
    plus_y = zpadded[:, 1:-1, 2:, 1:-1]
    minus_y = zpadded[:, 1:-1, :-2, 1:-1]
    plus_z = zpadded[:, 1:-1, 1:-1, 2:]
    minus_z = zpadded[:, 1:-1, 1:-1, :-2]
    slopes = ((plus_x - minus_x) * 0.5, (plus_y - minus_y) * 0.5, (plus_z - minus_z) * 0.5)
    laplace = plus_x + minus_x + plus_y + minus_y + plus_z + minus_z - 6.0 * center
    return center, slopes, laplace


def advance(padded, velocity, vel_slopes, source):
    center, slopes, laplace = derivatives(padded)
    carried = velocity[0] * slopes[0] + velocity[1] * slopes[1] + velocity[2] * slopes[2]
    stretched = center[0] * vel_slopes[0] + center[1] * vel_slopes[1] + center[2] * vel_slopes[2]
    return center + time_step * (stretched - carried + source) + viscous * laplace


def deposit_step(sources, incidence, azimuth, step):
    chosen = incidence[azimuth[step]]
    counts = jnp.sum(chosen[:, :, None] == jnp.arange(NSRC, dtype=jnp.int32)[None, None, :], axis=1).astype(jnp.bfloat16)
    flat = jnp.dot(counts, sources.reshape(NSRC, -1), preferred_element_type=jnp.float32)
    return flat.reshape(NX, 3, NY, NZ).transpose(1, 0, 2, 3)


def reference(vorticity, velocity, sources, incidence, azimuth):
    vel_pad = jnp.pad(velocity, ((0, 0), (1, 1), (1, 1), (0, 0)))
    unused, vel_slopes, unused_lap = derivatives(vel_pad)
    field = vorticity
    for step in range(STEPS):
        padded = jnp.pad(field, ((0, 0), (1, 1), (1, 1), (0, 0)))
        field = advance(padded, velocity, vel_slopes, deposit_step(sources, incidence, azimuth, step))
    return field
```

```python
import functools

import jax
import jax.numpy as jnp
from jax import lax
from jax.experimental import pallas as pl
from jax.experimental.pallas import tpu as pltpu
from jax.sharding import PartitionSpec as P

time_step = 0.2
viscous = 0.1
slope = 0.5 * time_step

LANES = 128
ROWS = 8
VMEM = pl.BlockSpec(memory_space=pltpu.VMEM)
SMEM = pl.BlockSpec(memory_space=pltpu.SMEM)
f32 = jnp.float32
f16 = jnp.float16

velocity_scale = 2.0**13
field_scales = (2.0**13, 2.0**10, 2.0**8)


def in_vmem(x):
    return pltpu.with_memory_space_constraint(x, pltpu.VMEM)


def call(kernel, outs, *args, smem=1, aliases=None, cost=None):
    args = args[:smem] + tuple(in_vmem(a) for a in args[smem:])
    multiple = isinstance(outs, list)
    return pl.pallas_call(
        kernel,
        out_shape=[pltpu.VMEM(o.shape, o.dtype) for o in outs] if multiple else pltpu.VMEM(outs.shape, outs.dtype),
        in_specs=[SMEM] * smem + [VMEM] * (len(args) - smem),
        out_specs=[VMEM] * len(outs) if multiple else VMEM,
        input_output_aliases=aliases or {},
        compiler_params=pltpu.CompilerParams(vmem_limit_bytes=16 * 1024 * 1024),
        cost_estimate=pl.CostEstimate(flops=cost, bytes_accessed=cost // 4, transcendentals=0) if cost else None,
    )(*args)


def pack_planes(pos, field, scale, out_refs, first):
    even = pos[0] == 0
    last = field.shape[1] - 1
    toward_first = jnp.where(even, last, 0)
    for out, plane in ((out_refs[0], toward_first), (out_refs[1], last - toward_first)):
        for c in range(3):
            out[first + c] = field[c, plane] * scale


def pack_rows(pos, field, out_refs, first):
    even = pos[1] == 0
    for c in range(3):
        low = field[c, :, 0, :]
        high = field[c, :, field.shape[2] - 1, :]
        out_refs[0][first + c] = jnp.where(even, high, low)
        out_refs[1][first + c] = jnp.where(even, low, high)


def pack_kernel(pos, w, v, x1, x2, y1, y2):
    pack_planes(pos, w, field_scales[0], (x1, x2), 0)
    pack_planes(pos, v, velocity_scale, (x1, x2), 3)
    pack_rows(pos, w, (y1, y2), 0)
    pack_rows(pos, v, (y1, y2), 3)


def gather_kernel(blocks, stages, pos, *refs):
    *parts, table = refs
    z = pos[2]
    toward = 1 - 2 * pos[0]
    per = parts[0].shape[0]

    def put(part, owner):
        for b in range(per):
            table[owner * per + b] = part[b].astype(f32) * time_step

    put(parts[0], z)
    for stage in range(1, stages):
        for part, way in ((parts[2 * stage - 1], toward), (parts[2 * stage], -toward)):
            owner = z + way * stage
            pl.when((owner >= 0) & (owner < stages))(functools.partial(put, part, owner))
    table[blocks] = jnp.zeros(table.shape[1:], f32)


def shifted(parts, lane, up):
    out = []
    for i, part in enumerate(parts):
        other = i + 1 if up else i - 1
        edge = pltpu.roll(parts[other], LANES - 1 if up else 1, 1) if 0 <= other < len(parts) else 0.0
        own = pltpu.roll(part, LANES - 1 if up else 1, 1)
        out.append(jnp.where(lane == (LANES - 1 if up else 0), edge, own))
    return out


def local_kernel(step, slots, ids, w, v, *refs):
    if step:
        table, out = refs
    else:
        (out,) = refs
    planes, rows, depth = w.shape[1:]
    slabs = depth // LANES
    lane = lax.broadcasted_iota(jnp.int32, (ROWS, LANES), 1)
    sub = lax.broadcasted_iota(jnp.int32, (ROWS, LANES), 0)

    def plane_body(x, _):
        before = jnp.maximum(x - 1, 0)
        after = jnp.minimum(x + 1, planes - 1)
        low = jnp.where(x > 0, slope, 0.0)
        high = jnp.where(x < planes - 1, slope, 0.0)

        def piece(ref, first, second, j, s):
            return ref[first, second, j * ROWS : (j + 1) * ROWS, s * LANES : (s + 1) * LANES]

        def around(ref, c, j):
            centre = [piece(ref, c, x, j, s) for s in range(slabs)]
            up_z = shifted(centre, lane, True)
            down_z = shifted(centre, lane, False)
            up_y, down_y = [], []
            for s in range(slabs):
                nxt = piece(ref, c, x, j + 1, s) if (j + 1) * ROWS < rows else 0.0
                prv = piece(ref, c, x, j - 1, s) if j else 0.0
                up_y.append(pltpu.roll(jnp.where(sub == 0, nxt, centre[s]), ROWS - 1, 0))
                down_y.append(pltpu.roll(jnp.where(sub == ROWS - 1, prv, centre[s]), 1, 0))
            up_x = [piece(ref, c, after, j, s) for s in range(slabs)]
            down_x = [piece(ref, c, before, j, s) for s in range(slabs)]
            return centre, up_x, down_x, up_y, down_y, up_z, down_z

        for j in range(rows // ROWS):
            vel = [around(v, c, j) for c in range(3)]
            fld = [around(w, c, j) for c in range(3)]
            for s in range(slabs):
                v0, v1, v2 = (vel[c][0][s] for c in range(3))
                up_x = high - high * v0
                down_x = low + low * v0
                p1, p2 = slope * v1, slope * v2
                up_y, down_y = slope - p1, slope + p1
                up_z, down_z = slope - p2, slope + p2
                w0 = fld[0][0][s]
                w0_up, w0_down = high * w0, low * w0
                w1, w2 = slope * fld[1][0][s], slope * fld[2][0][s]
                for c in range(3):
                    centre, ux, dx, uy, dy, uz, dz = (a[s] for a in fld[c])
                    vc, vux, vdx, vuy, vdy, vuz, vdz = (a[s] for a in vel[c])
                    total = (1.0 - 6.0 * viscous) * centre
                    total += up_x * ux + down_x * dx
                    total += up_y * uy + down_y * dy
                    total += up_z * uz + down_z * dz
                    total += w0_up * vux - w0_down * vdx
                    total += w1 * (vuy - vdy) + w2 * (vuz - vdz)
                    if step:
                        for k in range(slots):
                            block = ids[(step * planes + x) * slots + k]
                            total += piece(table, block, c, j, s)
                    out[c, x, j * ROWS : (j + 1) * ROWS, s * LANES : (s + 1) * LANES] = total
        return 0

    lax.fori_loop(0, planes, plane_body, 0)


def fix_kernel(step, slots, final, *refs):
    if step:
        pos, new, w, v, x1, x2, vx1, vx2, y1, y2, vy1, vy2, out, *sends = refs
        off = 0
    else:
        pos, ids, new, w, v, x1, x2, y1, y2, table, out, *sends = refs
        vx1, vx2, vy1, vy2 = x1, x2, y1, y2
    planes, rows = new.shape[1:3]
    last = planes - 1
    even_x, even_y = pos[0] == 0, pos[1] == 0

    if not step:

        def deposit(x, _):
            for k in range(slots):
                block = ids[x * slots + k]
                for c in range(3):
                    out[c, x] = new[c, x] + table[block, c] if k == 0 else out[c, x] + table[block, c]
            return 0

        lax.fori_loop(0, planes, deposit, 0)
        base = out
    else:
        base = new

    toward_first = jnp.where(even_x, last, 0)
    sign_first = jnp.where(even_x, -slope, slope)
    unscale = 1.0 / field_scales[step]
    v_unscale = 1.0 / velocity_scale
    for halo, v_halo, plane, sign in (
        (x1, vx1, toward_first, sign_first),
        (x2, vx2, last - toward_first, -sign_first),
    ):
        coef = slope + sign * v[0, plane]
        stretch = (-sign * v_unscale) * w[0, plane]
        coef = coef * unscale
        for c in range(3):
            out[c, plane] = base[c, plane] + coef * halo[c] + stretch * v_halo[3 + c]

    for low in (True, False):
        row = 0 if low else rows - 1
        sign = slope if low else -slope
        first = even_y if not low else jnp.logical_not(even_y)
        coef = slope + sign * v[1, :, row, :]
        stretch = -sign * w[1, :, row, :]
        for c in range(3):
            halo = jnp.where(first, y1[c], y2[c])
            v_halo = jnp.where(first, vy1[3 + c], vy2[3 + c])
            out[c, :, row, :] = out[c, :, row, :] + coef * halo + stretch * v_halo

    if not final:
        px1, px2, py1, py2 = sends
        pack_planes(pos, out, field_scales[step + 1], (px1, px2), 0)
        pack_rows(pos, out, (py1, py2), 0)


def swaps(axis):
    count = lax.axis_size(axis)
    pairs = []
    for start in (0, 1):
        both = []
        for i in range(start, count - 1, 2):
            both += [(i, i + 1), (i + 1, i)]
        pairs.append(both)
    return pairs


def per_device(vorticity, velocity, sources, incidence, azimuth):
    planes, rows, depth = vorticity.shape[1:]
    steps = azimuth.shape[0]
    slots = incidence.shape[2]
    count = lax.axis_size("xz")
    blocks = count * sources.shape[0]
    z = lax.axis_index("xz")
    y = lax.axis_index("gy")
    pos = jnp.stack([z % 2, y % 2, z]).astype(jnp.int32)
    chosen = incidence[azimuth]
    ids = lax.dynamic_slice_in_dim(chosen, z * planes, planes, 1).reshape(-1)
    ids = jnp.clip(ids, 0, blocks)
    x_pairs, y_pairs = swaps("xz"), swaps("gy")

    def shape(*dims, dtype=f32):
        return jax.ShapeDtypeStruct(dims, dtype)

    def swap_x(a, which):
        return lax.ppermute(a, "xz", x_pairs[which])

    def swap_planes(pair):
        return [swap_x(a.astype(f16), i).astype(f32) for i, a in enumerate(pair)]

    def swap_rows(pair):
        return [lax.ppermute(a, "gy", y_pairs[i]) for i, a in enumerate(pair)]

    work = 3 * planes * rows * depth * 40
    whole = shape(3, planes, rows, depth)
    sends = call(
        pack_kernel, [shape(6, rows, depth)] * 2 + [shape(6, planes, depth)] * 2, pos, vorticity, velocity
    )
    parts = [sources]
    came = [sources, sources]
    halo = swap_planes(sends[:2])
    side = swap_rows(sends[2:])
    for stage in range(1, count):
        came = [swap_x(came[1], 0), swap_x(came[0], 1)]
        parts += came
    table = call(
        functools.partial(gather_kernel, blocks, count), shape(blocks + 1, 3, rows, depth), pos, *parts
    )
    v_halo, v_side = halo, side
    field = vorticity
    for step in range(steps):
        final = step == steps - 1
        extra = [table] if step else []
        new = call(
            functools.partial(local_kernel, step, slots), whole, ids, field, velocity, *extra, cost=work
        )
        outs = [whole] + ([] if final else [shape(3, rows, depth)] * 2 + [shape(3, planes, depth)] * 2)
        fix = functools.partial(fix_kernel, step, slots, final)
        if step:
            result = call(
                fix, outs, pos, new, field, velocity, *halo, *v_halo, *side, *v_side, aliases={1: 0}, cost=work // 10
            )
        else:
            result = call(
                fix, outs, pos, ids, new, field, velocity, *halo, *side, table, smem=2, aliases={2: 0}, cost=work // 10
            )
        field = result[0]
        if not final:
            halo = swap_planes(result[1:3])
            side = swap_rows(result[3:5])
    return field


def solution(mesh):
    in_specs = (
        P(None, ("groups", "xz"), "gy", None),
        P(None, ("groups", "xz"), "gy", None),
        P(("groups", "xz"), None, "gy", None),
        P("groups", None, None),
        P("groups"),
    )
    out_specs = P(None, ("groups", "xz"), "gy", None)
    return jax.shard_map(
        per_device, mesh=mesh, in_specs=in_specs, out_specs=out_specs, check_vma=False
    )
```

```python
import functools

import jax
import jax.numpy as jnp
from jax import lax
from jax.experimental import pallas as pl
from jax.experimental.pallas import tpu as pltpu
from jax.sharding import PartitionSpec as P

time_step = 0.2
viscous = 0.1
slope = 0.5 * time_step

LANES = 128
ROWS = 8
VMEM = pl.BlockSpec(memory_space=pltpu.VMEM)
SMEM = pl.BlockSpec(memory_space=pltpu.SMEM)
HBM = pl.BlockSpec(memory_space=pl.ANY)
FIXED_HBM = pl.BlockSpec(memory_space=pltpu.HBM)
VMEM_LIMIT = 8 * 1024 * 1024
f32 = jnp.float32
f16 = jnp.float16

velocity_scale = 2.0**13
field_scales = (2.0**13, 2.0**10, 2.0**8)


def in_vmem(x):
    return pltpu.with_memory_space_constraint(x, pltpu.VMEM)


def in_hbm(x):
    return pltpu.with_memory_space_constraint(x, pltpu.HBM)


def call(kernel, outs, *args, smem=1, aliases=None, cost=None, hbm_out=False, scratch=()):
    specs = [SMEM] * smem + [VMEM] * (len(args) - smem)
    args = args[:smem] + tuple(in_vmem(a) for a in args[smem:])
    shapes = [pltpu.VMEM(o.shape, o.dtype) for o in outs]
    out_specs = [VMEM] * len(outs)
    if hbm_out:
        shapes[-1], out_specs[-1] = outs[-1], HBM
    return pl.pallas_call(
        kernel,
        out_shape=shapes,
        in_specs=specs,
        out_specs=out_specs,
        scratch_shapes=scratch,
        input_output_aliases=aliases or {},
        compiler_params=pltpu.CompilerParams(vmem_limit_bytes=VMEM_LIMIT),
        cost_estimate=pl.CostEstimate(flops=cost, bytes_accessed=cost // 4, transcendentals=0) if cost else None,
    )(*args)


def pack_planes(pos, field, out_refs):
    even = pos[0] == 0
    last = field.shape[1] - 1
    toward_first = jnp.where(even, last, 0)
    for out, plane in ((out_refs[0], toward_first), (out_refs[1], last - toward_first)):
        for c in range(3):
            out[c] = field[c, plane]


def pack_rows(pos, field, out_refs, first=0):
    even = pos[1] == 0
    for c in range(3):
        low = field[c, :, 0, :]
        high = field[c, :, field.shape[2] - 1, :]
        out_refs[0][first + c] = jnp.where(even, high, low)
        out_refs[1][first + c] = jnp.where(even, low, high)


def pack_planes_kernel(pos, w, v, x1, x2, sems):
    planes = w.shape[1]
    toward_first = jnp.where(pos[0] == 0, planes - 1, 0)
    copies = []
    for first, field in ((0, w), (3, v)):
        for out, plane in ((x1, toward_first), (x2, planes - 1 - toward_first)):
            one = pltpu.make_async_copy(field.at[:, plane], out.at[pl.ds(first, 3)], sems.at[len(copies)])
            one.start()
            copies.append(one)
    for one in copies:
        one.wait()


def pack_rows_kernel(pos, w, v, y1, y2):
    pack_rows(pos, w, (y1, y2), 0)
    pack_rows(pos, v, (y1, y2), 3)


def gather_kernel(slots, slot, order, pos, azimuth, incidence, field, *refs):
    *parts, table, out, py1, py2 = refs
    per = sum(part.shape[0] for part in parts) // len(order)
    places = [p * per + b for p in order for b in range(per)]
    for part in parts:
        for b in range(part.shape[0]):
            table[places.pop(0)] = part[b].astype(f32) * time_step
    table[table.shape[0] - 1] = jnp.zeros(table.shape[1:], f32)

    def deposit(x, _):
        where = [slot(pos, azimuth, incidence, 0, x, k) for k in range(slots)]
        for c in range(3):
            total = field[c, x]
            for block in where:
                total += table[block, c]
            out[c, x] = total
        return 0

    lax.fori_loop(0, out.shape[1], deposit, 0)
    pack_rows(pos, out, (py1, py2))


def slot_of_table(blocks, per, pos, azimuth, incidence, step, plane, k):
    plane = jnp.clip(pos[2] + plane, 0, incidence.shape[2] - 1)
    block = incidence[azimuth[step], k, plane]
    owner = block // per if per > 1 else block
    slot = (owner ^ pos[3]) * per + block % per if per > 1 else owner ^ pos[3]
    return jnp.where((block >= 0) & (block < blocks), slot, blocks)


def shifted(parts, lane, up):
    out = []
    for i, part in enumerate(parts):
        other = i + 1 if up else i - 1
        edge = pltpu.roll(parts[other], LANES - 1 if up else 1, 1) if 0 <= other < len(parts) else 0.0
        own = pltpu.roll(part, LANES - 1 if up else 1, 1)
        out.append(jnp.where(lane == (LANES - 1 if up else 0), edge, own))
    return out


def local_kernel(step, slots, slot, pos, azimuth, incidence, w, v, *refs):
    if step:
        table, grad, out = refs
    else:
        out, grad = refs
    planes, rows, depth = w.shape[1:]
    slabs = range(depth // LANES)
    chunks = rows // ROWS
    lane = lax.broadcasted_iota(jnp.int32, (ROWS, LANES), 1)
    sub = lax.broadcasted_iota(jnp.int32, (ROWS, LANES), 0)
    comps = range(3)

    def plane_body(x, _):
        before = jnp.maximum(x - 1, 0)
        after = jnp.minimum(x + 1, planes - 1)
        low = jnp.where(x > 0, slope, 0.0)
        high = jnp.where(x < planes - 1, slope, 0.0)
        deposits = [slot(pos, azimuth, incidence, step, x, k) for k in range(slots)] if step else []

        def place(j, s):
            return slice(j * ROWS, (j + 1) * ROWS), slice(s * LANES, (s + 1) * LANES)

        def load(ref, plane, j):
            return [[ref[(c, plane, *place(j, s))] for s in slabs] for c in comps]

        def along_y(prv, cur, nxt):
            up = pltpu.roll(jnp.where(sub == 0, 0.0 if nxt is None else nxt, cur), ROWS - 1, 0)
            down = pltpu.roll(jnp.where(sub == ROWS - 1, 0.0 if prv is None else prv, cur), 1, 0)
            return up, down

        def pick(window, c, s):
            return [None if a is None else a[c][s] for a in window]

        fld = [None, None, load(w, x, 0)]
        vel = [None, None, load(v, x, 0)]
        for j in range(chunks):
            fld = fld[1:] + [load(w, x, j + 1) if j + 1 < chunks else None]
            vel = vel[1:] + [load(v, x, j + 1) if j + 1 < chunks else None]
            up_z = [shifted(fld[1][c], lane, True) for c in comps]
            down_z = [shifted(fld[1][c], lane, False) for c in comps]
            if not step:
                vel_up_z = [shifted(vel[1][c], lane, True) for c in comps]
                vel_down_z = [shifted(vel[1][c], lane, False) for c in comps]
            for s in slabs:
                v0, v1, v2 = (vel[1][c][s] for c in comps)
                x_up = high - high * v0
                x_down = low + low * v0
                p1, p2 = slope * v1, slope * v2
                y_up, y_down = slope - p1, slope + p1
                z_up, z_down = slope - p2, slope + p2
                w0, w1, w2 = (fld[1][c][s] for c in comps)
                for c in comps:
                    here = place(j, s)
                    if step:
                        g0, g1, g2 = (grad[(3 * i + c, x, *here)] for i in range(3))
                    else:
                        g0 = high * v[(c, after, *here)] - low * v[(c, before, *here)]
                        vuy, vdy = along_y(*pick(vel, c, s))
                        g1 = slope * (vuy - vdy)
                        g2 = slope * (vel_up_z[c][s] - vel_down_z[c][s])
                        for i, g in enumerate((g0, g1, g2)):
                            grad[(3 * i + c, x, *here)] = g
                    wuy, wdy = along_y(*pick(fld, c, s))
                    total = (1.0 - 6.0 * viscous) * fld[1][c][s]
                    total += (x_up * w[(c, after, *here)] + x_down * w[(c, before, *here)]) + (y_up * wuy + y_down * wdy)
                    total += (z_up * up_z[c][s] + z_down * down_z[c][s]) + (w0 * g0 + w1 * g1)
                    total += w2 * g2
                    for block in deposits:
                        total += table[(block, c, *here)]
                    out[(c, x, *here)] = total
        return 0

    lax.fori_loop(0, planes, plane_body, 0)


def fix_kernel(step, slots, slot, final, *refs):
    pos, azimuth, incidence, new, *refs = refs
    if step:
        if step == 1:
            table, *refs = refs
        v, x1, x2, y1, y2, out, *sends = refs
    else:
        grad, w, v, x1, x2, y1, y2, out, full, *sends = refs
    planes, rows = new.shape[1:3]
    last = planes - 1

    for low in (True, False):
        row = 0 if low else rows - 1
        there = jnp.where(pos[6 if low else 7] > 0, slope, 0.0)
        sign = there if low else -there
        first = (pos[1] == 0) if not low else (pos[1] != 0)
        coef = there + sign * v[1, :, row, :]
        for c in range(3):
            total = new[c, :, row, :] + coef * jnp.where(first, y1[c], y2[c])
            if not step:
                change = -sign * jnp.where(first, y1[3 + c], y2[3 + c])
                full[3 + c, :, row, :] = grad[3 + c, :, row, :] + change
                total += w[1, :, row, :] * change
            out[c, :, row, :] = total

    if final:
        result, sems = sends
        copies = [
            pltpu.make_async_copy(out.at[c, pl.ds(1, planes - 2)], result.at[c, pl.ds(1, planes - 2)], sems.at[c])
            for c in range(3)
        ]
        for one in copies:
            one.start()

    toward_first = jnp.where(pos[0] == 0, last, 0)
    unscale = 1.0 / field_scales[step]
    for which, halo, plane in ((0, x1, toward_first), (1, x2, last - toward_first)):
        there = jnp.where(pos[4 + which] > 0, slope, 0.0)
        sign = jnp.where(plane > 0, -there, there)
        if step == 1:
            beyond = jnp.where(plane > 0, planes, -1)
            blocks = [slot(pos, azimuth, incidence, 0, beyond, k) for k in range(slots)]
            coef = there + sign * v[0, plane]
        else:
            coef = (there * unscale) + (sign * unscale) * v[0, plane]
        for c in range(3):
            value = halo[c]
            if step == 1:
                value = value * unscale
                for block in blocks:
                    value += table[block, c]
            total = out[c, plane] + coef * value
            if not step:
                change = (-sign / velocity_scale) * halo[3 + c]
                full[c, plane] = grad[c, plane] + change
                total += w[0, plane] * change
            out[c, plane] = total

    if final:
        for i, plane in enumerate((0, last)):
            one = pltpu.make_async_copy(out.at[:, plane], result.at[:, plane], sems.at[3 + i])
            one.start()
            copies.append(one)
        for one in copies:
            one.wait()
    else:
        pack_planes(pos, out, sends[:2])
        if step:
            pack_rows(pos, out, sends[2:])


def swaps(axis, wrap):
    count = lax.axis_size(axis)
    pairs = []
    for start in (0, 1):
        both = []
        for i in range(count):
            other = ((i - start) ^ 1) + start
            if not 0 <= other < count:
                other = count - 1 - i if wrap and start and count % 2 == 0 else i
            both.append((i, other))
        pairs.append(both)
    return pairs


def gather_blocks(sources):
    count = lax.axis_size("xz")
    if count & (count - 1):
        return [lax.all_gather(sources, "xz", axis=0, tiled=True)], list(range(count))
    parts, order, stage = [sources], [0], count // 2
    while stage:
        payload = parts[0] if len(parts) == 1 else jnp.concatenate(parts, axis=0)
        parts.append(lax.ppermute(payload, "xz", [(i, i ^ stage) for i in range(count)]))
        order += [p ^ stage for p in order]
        stage //= 2
    return parts, order


def per_device(vorticity, velocity, sources, incidence, azimuth):
    planes, rows, depth = vorticity.shape[1:]
    steps = azimuth.shape[0]
    slots = incidence.shape[2]
    count, side_count = lax.axis_size("xz"), lax.axis_size("gy")
    per = sources.shape[0]
    blocks = count * per
    z = lax.axis_index("xz")
    y = lax.axis_index("gy")
    low_z, high_z = z > 0, z < count - 1
    pos = jnp.stack(
        [
            z % 2,
            y % 2,
            z * planes,
            0 if count & (count - 1) else z,
            jnp.where(z % 2 == 0, high_z, low_z),
            jnp.where(z % 2 == 0, low_z, high_z),
            y > 0,
            y < side_count - 1,
        ]
    ).astype(jnp.int32)
    incidence = jnp.transpose(incidence, (0, 2, 1))
    x_pairs, y_pairs = swaps("xz", False), swaps("gy", True)
    where = functools.partial(slot_of_table, blocks, per)

    def shape(*dims, dtype=f32):
        return jax.ShapeDtypeStruct(dims, dtype)

    def swap_planes(pair, scale):
        return [lax.ppermute((a * scale).astype(f16), "xz", x_pairs[i]).astype(f32) for i, a in enumerate(pair)]

    def swap_rows(pair):
        return [lax.ppermute(a, "gy", y_pairs[i]) for i, a in enumerate(pair)]

    work = 3 * planes * rows * depth * 40
    whole = shape(3, planes, rows, depth)
    parts, order = gather_blocks(sources)
    planes_out = pl.pallas_call(
        pack_planes_kernel,
        out_shape=[pltpu.VMEM((6, rows, depth), f32)] * 2,
        in_specs=[SMEM, FIXED_HBM, FIXED_HBM],
        out_specs=[VMEM] * 2,
        scratch_shapes=[pltpu.SemaphoreType.DMA((4,))],
        compiler_params=pltpu.CompilerParams(vmem_limit_bytes=VMEM_LIMIT),
    )(pos, in_hbm(vorticity), in_hbm(velocity))
    rows_out = call(pack_rows_kernel, [shape(6, planes, depth)] * 2, pos, vorticity, velocity)
    scale = jnp.array([field_scales[0]] * 3 + [velocity_scale] * 3, f32)[:, None, None]
    halo = swap_planes(planes_out, scale)
    side = swap_rows(rows_out)
    field = vorticity
    small = (pos, azimuth, incidence)
    grads = shape(9, planes, rows, depth)
    for step in range(steps):
        final = step == steps - 1
        local = functools.partial(local_kernel, step, slots, where)
        fix = functools.partial(fix_kernel, step, slots, where, final)
        send_x, send_y = [shape(3, rows, depth)] * 2, [shape(3, planes, depth)] * 2
        if step:
            (new,) = call(local, [whole], *small, field, velocity, table, grad, smem=3, cost=work)
            extra = [table] if step == 1 else []
            result = call(
                fix,
                [whole, whole] if final else [whole] + send_x + send_y,
                *small,
                new,
                *extra,
                velocity,
                *halo,
                *side,
                smem=3,
                aliases={3: 0},
                cost=work // 10,
                hbm_out=final,
                scratch=[pltpu.SemaphoreType.DMA((5,))] if final else (),
            )
            if final:
                return result[1]
            field = result[0]
            halo = swap_planes(result[1:3], field_scales[step + 1])
            side = swap_rows(result[3:5])
        else:
            new, grad = call(local, [whole, grads], *small, field, velocity, smem=3, cost=work)
            args = (new, grad, field, velocity, *halo, *side)
            new, grad, *ready = call(
                fix, [whole, grads] + send_x, *small, *args, smem=3, aliases={3: 0, 4: 1}, cost=work // 10
            )
            halo = swap_planes(ready, field_scales[1])
            table, field, *ready = call(
                functools.partial(gather_kernel, slots, where, order),
                [shape(blocks + 1, 3, rows, depth), whole] + send_y,
                *small,
                new,
                *parts,
                smem=3,
                aliases={3: 1},
                cost=work // 10,
            )
            side = swap_rows(ready)


def solution(mesh):
    in_specs = (
        P(None, ("groups", "xz"), "gy", None),
        P(None, ("groups", "xz"), "gy", None),
        P(("groups", "xz"), None, "gy", None),
        P("groups", None, None),
        P("groups"),
    )
    out_specs = P(None, ("groups", "xz"), "gy", None)
    return jax.shard_map(
        per_device, mesh=mesh, in_specs=in_specs, out_specs=out_specs, check_vma=False
    )
```

```python
import functools

import jax
import jax.numpy as jnp
from jax import lax
from jax.experimental import pallas as pl
from jax.experimental.pallas import tpu as pltpu
from jax.sharding import PartitionSpec as P

time_step = 0.2
viscous = 0.1
slope = 0.5 * time_step

LANES = 128
ROWS = 8
VMEM = pl.BlockSpec(memory_space=pltpu.VMEM)
SMEM = pl.BlockSpec(memory_space=pltpu.SMEM)
HBM = pl.BlockSpec(memory_space=pl.ANY)
FIXED_HBM = pl.BlockSpec(memory_space=pltpu.HBM)
VMEM_LIMIT = 8 * 1024 * 1024
f32 = jnp.float32
f16 = jnp.float16

velocity_scale = 2.0**13
field_scales = (2.0**13, 2.0**10, 2.0**8)


def in_vmem(x):
    return pltpu.with_memory_space_constraint(x, pltpu.VMEM)


def in_hbm(x):
    return pltpu.with_memory_space_constraint(x, pltpu.HBM)


def call(kernel, outs, *args, smem=1, aliases=None, cost=None, hbm_out=False, scratch=()):
    specs = [SMEM] * smem + [VMEM] * (len(args) - smem)
    args = args[:smem] + tuple(in_vmem(a) for a in args[smem:])
    shapes = [pltpu.VMEM(o.shape, o.dtype) for o in outs]
    out_specs = [VMEM] * len(outs)
    if hbm_out:
        shapes[-1], out_specs[-1] = outs[-1], HBM
    return pl.pallas_call(
        kernel,
        out_shape=shapes,
        in_specs=specs,
        out_specs=out_specs,
        scratch_shapes=scratch,
        input_output_aliases=aliases or {},
        compiler_params=pltpu.CompilerParams(vmem_limit_bytes=VMEM_LIMIT),
        cost_estimate=pl.CostEstimate(flops=cost, bytes_accessed=cost // 4, transcendentals=0) if cost else None,
    )(*args)


def pack_planes(pos, field, out_refs):
    even = pos[0] == 0
    last = field.shape[1] - 1
    toward_first = jnp.where(even, last, 0)
    for out, plane in ((out_refs[0], toward_first), (out_refs[1], last - toward_first)):
        for c in range(3):
            out[c] = field[c, plane]


def pack_rows(pos, field, out_refs, first=0):
    even = pos[1] == 0
    for c in range(3):
        low = field[c, :, 0, :]
        high = field[c, :, field.shape[2] - 1, :]
        out_refs[0][first + c] = jnp.where(even, high, low)
        out_refs[1][first + c] = jnp.where(even, low, high)


def pack_planes_kernel(pos, w, v, x1, x2, sems):
    planes = w.shape[1]
    toward_first = jnp.where(pos[0] == 0, planes - 1, 0)
    copies = []
    for first, field in ((0, w), (3, v)):
        for out, plane in ((x1, toward_first), (x2, planes - 1 - toward_first)):
            one = pltpu.make_async_copy(field.at[:, plane], out.at[pl.ds(first, 3)], sems.at[len(copies)])
            one.start()
            copies.append(one)
    for one in copies:
        one.wait()


def pack_rows_kernel(pos, w, v, y1, y2):
    pack_rows(pos, w, (y1, y2), 0)
    pack_rows(pos, v, (y1, y2), 3)


def gather_kernel(slots, slot, order, pos, azimuth, incidence, field, *refs):
    *parts, table, out, py1, py2 = refs
    per = sum(part.shape[0] for part in parts) // len(order)
    places = [p * per + b for p in order for b in range(per)]
    for part in parts:
        for b in range(part.shape[0]):
            table[places.pop(0)] = part[b].astype(f32) * time_step
    table[table.shape[0] - 1] = jnp.zeros(table.shape[1:], f32)

    def deposit(x, _):
        where = [slot(pos, azimuth, incidence, 0, x, k) for k in range(slots)]
        for c in range(3):
            total = field[c, x]
            for block in where:
                total += table[block, c]
            out[c, x] = total
        return 0

    lax.fori_loop(0, out.shape[1], deposit, 0)
    pack_rows(pos, out, (py1, py2))


def slot_of_table(blocks, per, pos, azimuth, incidence, step, plane, k):
    plane = jnp.clip(pos[2] + plane, 0, incidence.shape[2] - 1)
    block = incidence[azimuth[step], k, plane]
    owner = block // per if per > 1 else block
    slot = (owner ^ pos[3]) * per + block % per if per > 1 else owner ^ pos[3]
    return jnp.where((block >= 0) & (block < blocks), slot, blocks)


def shifted(parts, lane, up):
    out = []
    for i, part in enumerate(parts):
        other = i + 1 if up else i - 1
        edge = pltpu.roll(parts[other], LANES - 1 if up else 1, 1) if 0 <= other < len(parts) else 0.0
        own = pltpu.roll(part, LANES - 1 if up else 1, 1)
        out.append(jnp.where(lane == (LANES - 1 if up else 0), edge, own))
    return out


def local_kernel(step, slots, slot, pos, azimuth, incidence, w, v, *refs):
    if step:
        table, grad, out = refs
    else:
        out, grad = refs
    planes, rows, depth = w.shape[1:]
    slabs = range(depth // LANES)
    chunks = rows // ROWS
    lane = lax.broadcasted_iota(jnp.int32, (ROWS, LANES), 1)
    sub = lax.broadcasted_iota(jnp.int32, (ROWS, LANES), 0)
    comps = range(3)

    def plane_body(x, _):
        before = jnp.maximum(x - 1, 0)
        after = jnp.minimum(x + 1, planes - 1)
        low = jnp.where(x > 0, slope, 0.0)
        high = jnp.where(x < planes - 1, slope, 0.0)
        deposits = [slot(pos, azimuth, incidence, step, x, k) for k in range(slots)] if step else []

        def place(j, s):
            return slice(j * ROWS, (j + 1) * ROWS), slice(s * LANES, (s + 1) * LANES)

        def load(ref, plane, j):
            return [[ref[(c, plane, *place(j, s))] for s in slabs] for c in comps]

        def along_y(prv, cur, nxt):
            up = pltpu.roll(jnp.where(sub == 0, 0.0 if nxt is None else nxt, cur), ROWS - 1, 0)
            down = pltpu.roll(jnp.where(sub == ROWS - 1, 0.0 if prv is None else prv, cur), 1, 0)
            return up, down

        def pick(window, c, s):
            return [None if a is None else a[c][s] for a in window]

        fld = [None, None, load(w, x, 0)]
        vel = [None, None, load(v, x, 0)]
        for j in range(chunks):
            fld = fld[1:] + [load(w, x, j + 1) if j + 1 < chunks else None]
            vel = vel[1:] + [load(v, x, j + 1) if j + 1 < chunks else None]
            up_z = [shifted(fld[1][c], lane, True) for c in comps]
            down_z = [shifted(fld[1][c], lane, False) for c in comps]
            if not step:
                vel_up_z = [shifted(vel[1][c], lane, True) for c in comps]
                vel_down_z = [shifted(vel[1][c], lane, False) for c in comps]
            for s in slabs:
                v0, v1, v2 = (vel[1][c][s] for c in comps)
                x_up = high - high * v0
                x_down = low + low * v0
                p1, p2 = slope * v1, slope * v2
                y_up, y_down = slope - p1, slope + p1
                z_up, z_down = slope - p2, slope + p2
                w0, w1, w2 = (fld[1][c][s] for c in comps)
                for c in comps:
                    here = place(j, s)
                    if step:
                        g0, g1, g2 = (grad[(3 * i + c, x, *here)] for i in range(3))
                    else:
                        g0 = high * v[(c, after, *here)] - low * v[(c, before, *here)]
                        vuy, vdy = along_y(*pick(vel, c, s))
                        g1 = slope * (vuy - vdy)
                        g2 = slope * (vel_up_z[c][s] - vel_down_z[c][s])
                        terms = [g0, g1, g2]
                        terms[c] += 1.0 - 6.0 * viscous
                        g0, g1, g2 = terms
                        for i, g in enumerate(terms):
                            grad[(3 * i + c, x, *here)] = g
                    wuy, wdy = along_y(*pick(fld, c, s))
                    total = (x_up * w[(c, after, *here)] + x_down * w[(c, before, *here)]) + (y_up * wuy + y_down * wdy)
                    total += (z_up * up_z[c][s] + z_down * down_z[c][s]) + (w0 * g0 + w1 * g1)
                    total += w2 * g2
                    for block in deposits:
                        total += table[(block, c, *here)]
                    out[(c, x, *here)] = total
        return 0

    lax.fori_loop(0, planes, plane_body, 0)


def fix_kernel(step, slots, slot, final, *refs):
    pos, azimuth, incidence, new, *refs = refs
    if step:
        if step == 1:
            table, *refs = refs
        v, x1, x2, y1, y2, out, *sends = refs
    else:
        grad, w, v, x1, x2, y1, y2, out, full, *sends = refs
    planes, rows = new.shape[1:3]
    last = planes - 1
    inner = pl.ds(1, planes - 2)
    copies = []

    def write(source, target):
        copies.append(pltpu.make_async_copy(source, target, sems.at[len(copies)]))
        copies[-1].start()

    if final:
        result, sems = sends
        middle = pl.ds(ROWS, rows - 2 * ROWS)
        for c in range(3):
            write(out.at[c, inner, middle], result.at[c, inner, middle])

    for low in (True, False):
        row = 0 if low else rows - 1
        there = jnp.where(pos[6 if low else 7] > 0, slope, 0.0)
        sign = there if low else -there
        first = (pos[1] == 0) if not low else (pos[1] != 0)
        coef = there + sign * v[1, :, row, :]
        for c in range(3):
            total = new[c, :, row, :] + coef * jnp.where(first, y1[c], y2[c])
            if not step:
                change = -sign * jnp.where(first, y1[3 + c], y2[3 + c])
                full[3 + c, :, row, :] = grad[3 + c, :, row, :] + change
                total += w[1, :, row, :] * change
            out[c, :, row, :] = total

    if final:
        for c in range(3):
            for tile in (0, rows - ROWS):
                write(out.at[c, inner, pl.ds(tile, ROWS)], result.at[c, inner, pl.ds(tile, ROWS)])

    toward_first = jnp.where(pos[0] == 0, last, 0)
    unscale = 1.0 / field_scales[step]
    for which, halo, plane in ((0, x1, toward_first), (1, x2, last - toward_first)):
        there = jnp.where(pos[4 + which] > 0, slope, 0.0)
        sign = jnp.where(plane > 0, -there, there)
        if step == 1:
            beyond = jnp.where(plane > 0, planes, -1)
            blocks = [slot(pos, azimuth, incidence, 0, beyond, k) for k in range(slots)]
            coef = there + sign * v[0, plane]
        else:
            coef = (there * unscale) + (sign * unscale) * v[0, plane]
        for c in range(3):
            value = halo[c]
            if step == 1:
                value = value * unscale
                for block in blocks:
                    value += table[block, c]
            total = out[c, plane] + coef * value
            if not step:
                change = (-sign / velocity_scale) * halo[3 + c]
                full[c, plane] = grad[c, plane] + change
                total += w[0, plane] * change
            out[c, plane] = total

    if final:
        for plane in (0, last):
            write(out.at[:, plane], result.at[:, plane])
        for one in copies:
            one.wait()
    else:
        pack_planes(pos, out, sends[:2])
        if step:
            pack_rows(pos, out, sends[2:])


def swaps(axis, wrap):
    count = lax.axis_size(axis)
    pairs = []
    for start in (0, 1):
        both = []
        for i in range(count):
            other = ((i - start) ^ 1) + start
            if not 0 <= other < count:
                other = count - 1 - i if wrap and start and count % 2 == 0 else i
            both.append((i, other))
        pairs.append(both)
    return pairs


def gather_blocks(sources):
    count = lax.axis_size("xz")
    if count & (count - 1):
        return [lax.all_gather(sources, "xz", axis=0, tiled=True)], list(range(count))
    parts, order, stage = [sources], [0], count // 2
    while stage:
        payload = parts[0] if len(parts) == 1 else jnp.concatenate(parts, axis=0)
        parts.append(lax.ppermute(payload, "xz", [(i, i ^ stage) for i in range(count)]))
        order += [p ^ stage for p in order]
        stage //= 2
    return parts, order


def per_device(vorticity, velocity, sources, incidence, azimuth):
    planes, rows, depth = vorticity.shape[1:]
    steps = azimuth.shape[0]
    slots = incidence.shape[2]
    count, side_count = lax.axis_size("xz"), lax.axis_size("gy")
    per = sources.shape[0]
    blocks = count * per
    z = lax.axis_index("xz")
    y = lax.axis_index("gy")
    low_z, high_z = z > 0, z < count - 1
    pos = jnp.stack(
        [
            z % 2,
            y % 2,
            z * planes,
            0 if count & (count - 1) else z,
            jnp.where(z % 2 == 0, high_z, low_z),
            jnp.where(z % 2 == 0, low_z, high_z),
            y > 0,
            y < side_count - 1,
        ]
    ).astype(jnp.int32)
    incidence = jnp.transpose(incidence, (0, 2, 1))
    x_pairs, y_pairs = swaps("xz", False), swaps("gy", True)
    where = functools.partial(slot_of_table, blocks, per)

    def shape(*dims, dtype=f32):
        return jax.ShapeDtypeStruct(dims, dtype)

    def swap_planes(pair, scale):
        second, first = [lax.ppermute((pair[i] * scale).astype(f16), "xz", x_pairs[i]) for i in (1, 0)]
        return first, second

    def swap_rows(pair):
        return [lax.ppermute(a, "gy", y_pairs[i]) for i, a in enumerate(pair)]

    work = 3 * planes * rows * depth * 40
    whole = shape(3, planes, rows, depth)
    parts, order = gather_blocks(sources)
    planes_out = pl.pallas_call(
        pack_planes_kernel,
        out_shape=[pltpu.VMEM((6, rows, depth), f32)] * 2,
        in_specs=[SMEM, FIXED_HBM, FIXED_HBM],
        out_specs=[VMEM] * 2,
        scratch_shapes=[pltpu.SemaphoreType.DMA((4,))],
        compiler_params=pltpu.CompilerParams(vmem_limit_bytes=VMEM_LIMIT),
    )(pos, in_hbm(vorticity), in_hbm(velocity))
    vorticity, velocity, planes_out = lax.optimization_barrier((vorticity, velocity, planes_out))
    rows_out = call(pack_rows_kernel, [shape(6, planes, depth)] * 2, pos, vorticity, velocity)
    scale = jnp.array([field_scales[0]] * 3 + [velocity_scale] * 3, f32)[:, None, None]
    halo = swap_planes(planes_out, scale)
    side = swap_rows(rows_out)
    field = vorticity
    small = (pos, azimuth, incidence)
    grads = shape(9, planes, rows, depth)
    for step in range(steps):
        final = step == steps - 1
        local = functools.partial(local_kernel, step, slots, where)
        fix = functools.partial(fix_kernel, step, slots, where, final)
        send_x, send_y = [shape(3, rows, depth)] * 2, [shape(3, planes, depth)] * 2
        if step:
            (new,) = call(local, [whole], *small, field, velocity, table, grad, smem=3, cost=work)
            if step == 1:
                one, *side = lax.optimization_barrier((jnp.ones((1, 1, depth), f32), *side))
                halo = [a.astype(f32) * one for a in halo]
            else:
                halo = [a.astype(f32) for a in halo]
            extra = [table] if step == 1 else []
            result = call(
                fix,
                [whole, whole] if final else [whole] + send_x + send_y,
                *small,
                new,
                *extra,
                velocity,
                *halo,
                *side,
                smem=3,
                aliases={3: 0},
                cost=work // 10,
                hbm_out=final,
                scratch=[pltpu.SemaphoreType.DMA((11,))] if final else (),
            )
            if final:
                return result[1]
            field = result[0]
            halo = swap_planes(result[1:3], field_scales[step + 1])
            side = swap_rows(result[3:5])
        else:
            gate, parts[1] = lax.optimization_barrier((pos, parts[1]))
            new, grad = call(local, [whole, grads], gate, azimuth, incidence, field, velocity, smem=3, cost=work)
            args = (new, grad, field, velocity, *[a.astype(f32) for a in halo], *side)
            new, grad, *ready = call(
                fix, [whole, grads] + send_x, *small, *args, smem=3, aliases={3: 0, 4: 1}, cost=work // 10
            )
            halo = swap_planes(ready, field_scales[1])
            table, field, *ready = call(
                functools.partial(gather_kernel, slots, where, order),
                [shape(blocks + 1, 3, rows, depth), whole] + send_y,
                *small,
                new,
                *parts,
                smem=3,
                aliases={3: 1},
                cost=work // 10,
            )
            side = swap_rows(ready)


def solution(mesh):
    in_specs = (
        P(None, ("groups", "xz"), "gy", None),
        P(None, ("groups", "xz"), "gy", None),
        P(("groups", "xz"), None, "gy", None),
        P("groups", None, None),
        P("groups"),
    )
    out_specs = P(None, ("groups", "xz"), "gy", None)
    return jax.shard_map(
        per_device, mesh=mesh, in_specs=in_specs, out_specs=out_specs, check_vma=False
    )
```

```python
import functools

import jax
import jax.numpy as jnp
from jax import lax
from jax.experimental import pallas as pl
from jax.experimental.pallas import tpu as pltpu
from jax.sharding import PartitionSpec as P

time_step = 0.2
viscous = 0.1
slope = 0.5 * time_step

LANES = 128
ROWS = 8
VMEM = pl.BlockSpec(memory_space=pltpu.VMEM)
SMEM = pl.BlockSpec(memory_space=pltpu.SMEM)
HBM = pl.BlockSpec(memory_space=pl.ANY)
FIXED_HBM = pl.BlockSpec(memory_space=pltpu.HBM)
VMEM_LIMIT = 8 * 1024 * 1024
f32 = jnp.float32
f16 = jnp.float16

velocity_scale = 2.0**13
field_scales = (2.0**13, 2.0**10, 2.0**8)


def in_vmem(x):
    return pltpu.with_memory_space_constraint(x, pltpu.VMEM)


def in_hbm(x):
    return pltpu.with_memory_space_constraint(x, pltpu.HBM)


def call(kernel, outs, *args, smem=0, aliases=None, cost=None, hbm_out=False, scratch=()):
    specs = [SMEM] * smem + [VMEM] * (len(args) - smem)
    args = args[:smem] + tuple(in_vmem(a) for a in args[smem:])
    shapes = [pltpu.VMEM(o.shape, o.dtype) for o in outs]
    out_specs = [VMEM] * len(outs)
    if hbm_out:
        shapes[-1], out_specs[-1] = outs[-1], HBM
    return pl.pallas_call(
        kernel,
        out_shape=shapes,
        in_specs=specs,
        out_specs=out_specs,
        scratch_shapes=scratch,
        input_output_aliases=aliases or {},
        compiler_params=pltpu.CompilerParams(vmem_limit_bytes=VMEM_LIMIT),
        cost_estimate=pl.CostEstimate(flops=cost, bytes_accessed=cost // 4, transcendentals=0) if cost else None,
    )(*args)


def pack_planes(pos, field, out_refs, first=0):
    even = pos[0] == 0
    last = field.shape[1] - 1
    toward_first = jnp.where(even, last, 0)
    for out, plane in ((out_refs[0], toward_first), (out_refs[1], last - toward_first)):
        for c in range(3):
            out[first + c] = field[c, plane]


def pack_rows(pos, field, out_refs, first=0):
    even = pos[1] == 0
    for c in range(3):
        low = field[c, :, 0, :]
        high = field[c, :, field.shape[2] - 1, :]
        out_refs[0][first + c] = jnp.where(even, high, low)
        out_refs[1][first + c] = jnp.where(even, low, high)


def load_kernel(position, w_in, v_in, w, v, x1, x2, y1, y2, sems):
    pos = position()
    last = w.shape[1] - 1
    copies = []

    def load(source, target):
        copies.append(pltpu.make_async_copy(source, target, sems.at[len(copies)]))
        copies[-1].start()

    for source, target in ((w_in, w), (v_in, v)):
        for plane in (0, last):
            load(source.at[:, plane], target.at[:, plane])
    inner = pl.ds(1, last - 1)
    for source, target in ((w_in, w), (v_in, v)):
        for c in range(3):
            load(source.at[c, inner], target.at[c, inner])
    for one in copies[:4]:
        one.wait()
    pack_planes(pos, w, (x1, x2), 0)
    pack_planes(pos, v, (x1, x2), 3)
    for i, field in enumerate((w, v)):
        for one in copies[4 + 3 * i : 7 + 3 * i]:
            one.wait()
        pack_rows(pos, field, (y1, y2), 3 * i)


def gather_kernel(slots, slot, order, position, azimuth, incidence, field, *refs):
    *parts, table, out, py1, py2 = refs
    pos = position()
    per = sum(part.shape[0] for part in parts) // len(order)
    places = [p * per + b for p in order for b in range(per)]
    for part in parts:
        for b in range(part.shape[0]):
            table[places.pop(0)] = part[b].astype(f32) * time_step
    table[table.shape[0] - 1] = jnp.zeros(table.shape[1:], f32)

    def deposit(x, _):
        where = [slot(pos, azimuth, incidence, 0, x, k) for k in range(slots)]
        for c in range(3):
            total = field[c, x]
            for block in where:
                total += table[block, c]
            out[c, x] = total
        return 0

    lax.fori_loop(0, out.shape[1], deposit, 0)
    pack_rows(pos, out, (py1, py2))


def slot_of_table(blocks, per, pos, azimuth, incidence, step, plane, k):
    plane = jnp.clip(pos[2] + plane, 0, incidence.shape[2] - 1)
    block = incidence[azimuth[step], k, plane]
    owner = block // per if per > 1 else block
    slot = (owner ^ pos[3]) * per + block % per if per > 1 else owner ^ pos[3]
    return jnp.where((block >= 0) & (block < blocks), slot, blocks)


def shifted(parts, lane, up):
    out = []
    for i, part in enumerate(parts):
        other = i + 1 if up else i - 1
        edge = pltpu.roll(parts[other], LANES - 1 if up else 1, 1) if 0 <= other < len(parts) else 0.0
        own = pltpu.roll(part, LANES - 1 if up else 1, 1)
        out.append(jnp.where(lane == (LANES - 1 if up else 0), edge, own))
    return out


def local_kernel(step, slots, slot, position, *refs):
    if step:
        azimuth, incidence, w, v, table, grad, out = refs
        pos = position()
    else:
        w, v, out, grad = refs
    planes, rows, depth = w.shape[1:]
    slabs = range(depth // LANES)
    chunks = rows // ROWS
    lane = lax.broadcasted_iota(jnp.int32, (ROWS, LANES), 1)
    sub = lax.broadcasted_iota(jnp.int32, (ROWS, LANES), 0)
    comps = range(3)

    def plane_body(x, _):
        before = jnp.maximum(x - 1, 0)
        after = jnp.minimum(x + 1, planes - 1)
        low = jnp.where(x > 0, slope, 0.0)
        high = jnp.where(x < planes - 1, slope, 0.0)
        deposits = [slot(pos, azimuth, incidence, step, x, k) for k in range(slots)] if step else []

        def place(j, s):
            return slice(j * ROWS, (j + 1) * ROWS), slice(s * LANES, (s + 1) * LANES)

        def load(ref, plane, j):
            return [[ref[(c, plane, *place(j, s))] for s in slabs] for c in comps]

        def along_y(prv, cur, nxt):
            up = pltpu.roll(jnp.where(sub == 0, 0.0 if nxt is None else nxt, cur), ROWS - 1, 0)
            down = pltpu.roll(jnp.where(sub == ROWS - 1, 0.0 if prv is None else prv, cur), 1, 0)
            return up, down

        def pick(window, c, s):
            return [None if a is None else a[c][s] for a in window]

        fld = [None, None, load(w, x, 0)]
        vel = [None, None, load(v, x, 0)]
        for j in range(chunks):
            fld = fld[1:] + [load(w, x, j + 1) if j + 1 < chunks else None]
            vel = vel[1:] + [load(v, x, j + 1) if j + 1 < chunks else None]
            up_z = [shifted(fld[1][c], lane, True) for c in comps]
            down_z = [shifted(fld[1][c], lane, False) for c in comps]
            if not step:
                vel_up_z = [shifted(vel[1][c], lane, True) for c in comps]
                vel_down_z = [shifted(vel[1][c], lane, False) for c in comps]
            for s in slabs:
                v0, v1, v2 = (vel[1][c][s] for c in comps)
                x_up = high - high * v0
                x_down = low + low * v0
                p1, p2 = slope * v1, slope * v2
                y_up, y_down = slope - p1, slope + p1
                z_up, z_down = slope - p2, slope + p2
                w0, w1, w2 = (fld[1][c][s] for c in comps)
                for c in comps:
                    here = place(j, s)
                    if step:
                        g0, g1, g2 = (grad[(3 * i + c, x, *here)] for i in range(3))
                    else:
                        g0 = high * v[(c, after, *here)] - low * v[(c, before, *here)]
                        vuy, vdy = along_y(*pick(vel, c, s))
                        g1 = slope * (vuy - vdy)
                        g2 = slope * (vel_up_z[c][s] - vel_down_z[c][s])
                        terms = [g0, g1, g2]
                        terms[c] += 1.0 - 6.0 * viscous
                        g0, g1, g2 = terms
                        for i, g in enumerate(terms):
                            grad[(3 * i + c, x, *here)] = g
                    wuy, wdy = along_y(*pick(fld, c, s))
                    total = (x_up * w[(c, after, *here)] + x_down * w[(c, before, *here)]) + (y_up * wuy + y_down * wdy)
                    total += (z_up * up_z[c][s] + z_down * down_z[c][s]) + (w0 * g0 + w1 * g1)
                    total += w2 * g2
                    for block in deposits:
                        total += table[(block, c, *here)]
                    out[(c, x, *here)] = total
        return 0

    lax.fori_loop(0, planes, plane_body, 0)


def fix_kernel(step, slots, slot, position, final, *refs):
    if step == 1:
        azimuth, incidence, *refs = refs
    pos = position()
    new, *refs = refs
    if step:
        if step == 1:
            table, *refs = refs
        v, x1, x2, y1, y2, out, *sends = refs
    else:
        grad, w, v, x1, x2, y1, y2, out, full, *sends = refs
    planes, rows = new.shape[1:3]
    last = planes - 1
    inner = pl.ds(1, planes - 2)
    copies = []

    def write(source, target):
        copies.append(pltpu.make_async_copy(source, target, sems.at[len(copies)]))
        copies[-1].start()

    if final:
        result, sems = sends
        middle = pl.ds(ROWS, rows - 2 * ROWS)
        for c in range(3):
            write(out.at[c, inner, middle], result.at[c, inner, middle])

    for low in (True, False):
        row = 0 if low else rows - 1
        there = jnp.where(pos[6 if low else 7] > 0, slope, 0.0)
        sign = there if low else -there
        first = (pos[1] == 0) if not low else (pos[1] != 0)
        coef = there + sign * v[1, :, row, :]
        for c in range(3):
            total = new[c, :, row, :] + coef * jnp.where(first, y1[c], y2[c])
            if not step:
                change = -sign * jnp.where(first, y1[3 + c], y2[3 + c])
                full[3 + c, :, row, :] = grad[3 + c, :, row, :] + change
                total += w[1, :, row, :] * change
            out[c, :, row, :] = total

    if final:
        for c in range(3):
            for tile in (0, rows - ROWS):
                write(out.at[c, inner, pl.ds(tile, ROWS)], result.at[c, inner, pl.ds(tile, ROWS)])

    toward_first = jnp.where(pos[0] == 0, last, 0)
    unscale = 1.0 / field_scales[step]
    for which, halo, plane in ((0, x1, toward_first), (1, x2, last - toward_first)):
        there = jnp.where(pos[4 + which] > 0, slope, 0.0)
        sign = jnp.where(plane > 0, -there, there)
        if step == 1:
            beyond = jnp.where(plane > 0, planes, -1)
            blocks = [slot(pos, azimuth, incidence, 0, beyond, k) for k in range(slots)]
            coef = there + sign * v[0, plane]
        else:
            coef = (there * unscale) + (sign * unscale) * v[0, plane]
        for c in range(3):
            value = halo[c]
            if step == 1:
                value = value * unscale
                for block in blocks:
                    value += table[block, c]
            total = out[c, plane] + coef * value
            if not step:
                change = (-sign / velocity_scale) * halo[3 + c]
                full[c, plane] = grad[c, plane] + change
                total += w[0, plane] * change
            out[c, plane] = total

    if final:
        for plane in (0, last):
            write(out.at[:, plane], result.at[:, plane])
        for one in copies:
            one.wait()
    else:
        pack_planes(pos, out, sends[:2])
        if step:
            pack_rows(pos, out, sends[2:])


def swaps(axis, wrap):
    count = lax.axis_size(axis)
    pairs = []
    for start in (0, 1):
        both = []
        for i in range(count):
            other = ((i - start) ^ 1) + start
            if not 0 <= other < count:
                other = count - 1 - i if wrap and start and count % 2 == 0 else i
            both.append((i, other))
        pairs.append(both)
    return pairs


def gather_blocks(sources):
    count = lax.axis_size("xz")
    if count & (count - 1):
        return [lax.all_gather(sources, "xz", axis=0, tiled=True)], list(range(count))
    parts, order, stage = [sources], [0], count // 2
    while stage:
        payload = parts[0] if len(parts) == 1 else jnp.concatenate(parts, axis=0)
        parts.append(lax.ppermute(payload, "xz", [(i, i ^ stage) for i in range(count)]))
        order += [p ^ stage for p in order]
        stage //= 2
    return parts, order


def per_device(vorticity, velocity, sources, incidence, azimuth):
    planes, rows, depth = vorticity.shape[1:]
    steps = azimuth.shape[0]
    slots = incidence.shape[2]
    count, side_count = lax.axis_size("xz"), lax.axis_size("gy")
    per = sources.shape[0]
    blocks = count * per

    def position():
        z, y = lax.axis_index("xz"), lax.axis_index("gy")
        even = z % 2 == 0
        low, high = (z > 0).astype(jnp.int32), (z < count - 1).astype(jnp.int32)
        return [
            z % 2,
            y % 2,
            z * planes,
            0 if count & (count - 1) else z,
            jnp.where(even, high, low),
            jnp.where(even, low, high),
            (y > 0).astype(jnp.int32),
            (y < side_count - 1).astype(jnp.int32),
        ]

    incidence = jnp.transpose(incidence, (0, 2, 1))
    x_pairs, y_pairs = swaps("xz", False), swaps("gy", True)
    where = functools.partial(slot_of_table, blocks, per)

    def shape(*dims, dtype=f32):
        return jax.ShapeDtypeStruct(dims, dtype)

    def swap_planes(pair, scale):
        second, first = [lax.ppermute((pair[i] * scale).astype(f16), "xz", x_pairs[i]) for i in (1, 0)]
        return first, second

    def swap_rows(pair):
        return [lax.ppermute(a, "gy", y_pairs[i]) for i, a in enumerate(pair)]

    work = 3 * planes * rows * depth * 40
    whole = shape(3, planes, rows, depth)
    parts, order = gather_blocks(sources)
    vorticity, velocity, *sends = pl.pallas_call(
        functools.partial(load_kernel, position),
        out_shape=[pltpu.VMEM(whole.shape, f32)] * 2
        + [pltpu.VMEM((6, rows, depth), f32)] * 2
        + [pltpu.VMEM((6, planes, depth), f32)] * 2,
        in_specs=[FIXED_HBM, FIXED_HBM],
        out_specs=[VMEM] * 6,
        scratch_shapes=[pltpu.SemaphoreType.DMA((10,))],
        compiler_params=pltpu.CompilerParams(vmem_limit_bytes=VMEM_LIMIT),
    )(in_hbm(vorticity), in_hbm(velocity))
    scale = jnp.array([field_scales[0]] * 3 + [velocity_scale] * 3, f32)[:, None, None]
    halo = swap_planes(sends[:2], scale)
    side = swap_rows(sends[2:])
    field = vorticity
    small = (azimuth, incidence)
    grads = shape(9, planes, rows, depth)
    send_x, send_y = [shape(3, rows, depth)] * 2, [shape(3, planes, depth)] * 2
    for step in range(steps):
        final = step == steps - 1
        local = functools.partial(local_kernel, step, slots, where, position)
        fix = functools.partial(fix_kernel, step, slots, where, position, final)
        if step:
            (new,) = call(local, [whole], *small, field, velocity, table, grad, smem=2, cost=work)
            first = step == 1
            if first:
                one, *side = lax.optimization_barrier((jnp.ones((1, 1, depth), f32), *side))
                halo = [a.astype(f32) * one for a in halo]
            else:
                halo = [a.astype(f32) for a in halo]
            result = call(
                fix,
                [whole, whole] if final else [whole] + send_x + send_y,
                *(small if first else ()),
                new,
                *([table] if first else []),
                velocity,
                *halo,
                *side,
                smem=2 if first else 0,
                aliases={2 if first else 0: 0},
                cost=work // 10,
                hbm_out=final,
                scratch=[pltpu.SemaphoreType.DMA((11,))] if final else (),
            )
            if final:
                return result[1]
            field = result[0]
            halo = swap_planes(result[1:3], field_scales[step + 1])
            side = swap_rows(result[3:5])
        else:
            held, parts[1] = lax.optimization_barrier((field, parts[1]))
            new, grad = call(local, [whole, grads], held, velocity, cost=work)
            args = (new, grad, field, velocity, *[a.astype(f32) for a in halo], *side)
            new, grad, *ready = call(fix, [whole, grads] + send_x, *args, aliases={0: 0, 1: 1}, cost=work // 10)
            halo = swap_planes(ready, field_scales[1])
            table, field, *ready = call(
                functools.partial(gather_kernel, slots, where, order, position),
                [shape(blocks + 1, 3, rows, depth), whole] + send_y,
                *small,
                new,
                *parts,
                smem=2,
                aliases={2: 1},
                cost=work // 10,
            )
            side = swap_rows(ready)


def solution(mesh):
    in_specs = (
        P(None, ("groups", "xz"), "gy", None),
        P(None, ("groups", "xz"), "gy", None),
        P(("groups", "xz"), None, "gy", None),
        P("groups", None, None),
        P("groups"),
    )
    out_specs = P(None, ("groups", "xz"), "gy", None)
    return jax.shard_map(
        per_device, mesh=mesh, in_specs=in_specs, out_specs=out_specs, check_vma=False
    )
```

```python
import functools

import jax
import jax.numpy as jnp
from jax import lax
from jax.experimental import pallas as pl
from jax.experimental.pallas import tpu as pltpu
from jax.sharding import PartitionSpec as P

time_step = 0.2
viscous = 0.1
slope = 0.5 * time_step

LANES = 128
ROWS = 8
VMEM = pl.BlockSpec(memory_space=pltpu.VMEM)
SMEM = pl.BlockSpec(memory_space=pltpu.SMEM)
HBM = pl.BlockSpec(memory_space=pl.ANY)
FIXED_HBM = pl.BlockSpec(memory_space=pltpu.HBM)
VMEM_LIMIT = 8 * 1024 * 1024
f32 = jnp.float32
f16 = jnp.float16

velocity_scale = 2.0**13
field_scales = (2.0**13, 2.0**10, 2.0**8)


def in_vmem(x):
    return pltpu.with_memory_space_constraint(x, pltpu.VMEM)


def in_hbm(x):
    return pltpu.with_memory_space_constraint(x, pltpu.HBM)


def call(kernel, outs, *args, smem=0, aliases=None, cost=None, hbm_out=False, scratch=()):
    specs = [SMEM] * smem + [VMEM] * (len(args) - smem)
    args = args[:smem] + tuple(in_vmem(a) for a in args[smem:])
    shapes = [pltpu.VMEM(o.shape, o.dtype) for o in outs]
    out_specs = [VMEM] * len(outs)
    if hbm_out:
        shapes[-1], out_specs[-1] = outs[-1], HBM
    return pl.pallas_call(
        kernel,
        out_shape=shapes,
        in_specs=specs,
        out_specs=out_specs,
        scratch_shapes=scratch,
        input_output_aliases=aliases or {},
        compiler_params=pltpu.CompilerParams(vmem_limit_bytes=VMEM_LIMIT),
        cost_estimate=pl.CostEstimate(flops=cost, bytes_accessed=cost // 4, transcendentals=0) if cost else None,
    )(*args)


def pack_planes(pos, field, out_refs, first=0):
    even = pos[0] == 0
    last = field.shape[1] - 1
    toward_first = jnp.where(even, last, 0)
    for out, plane in ((out_refs[0], toward_first), (out_refs[1], last - toward_first)):
        for c in range(3):
            out[first + c] = field[c, plane]


def pack_rows(pos, field, out_refs, first=0):
    even = pos[1] == 0
    for c in range(3):
        low = field[c, :, 0, :]
        high = field[c, :, field.shape[2] - 1, :]
        out_refs[0][first + c] = jnp.where(even, high, low)
        out_refs[1][first + c] = jnp.where(even, low, high)


def load_kernel(position, w_in, v_in, w, v, x1, x2, y1, y2, sems):
    pos = position()
    last = w.shape[1] - 1
    copies = []

    def load(source, target):
        copies.append(pltpu.make_async_copy(source, target, sems.at[len(copies)]))
        copies[-1].start()

    for source, target in ((w_in, w), (v_in, v)):
        for plane in (0, last):
            load(source.at[:, plane], target.at[:, plane])
    inner = pl.ds(1, last - 1)
    for source, target in ((w_in, w), (v_in, v)):
        for c in range(3):
            load(source.at[c, inner], target.at[c, inner])
    for one in copies[:4]:
        one.wait()
    pack_planes(pos, w, (x1, x2), 0)
    pack_planes(pos, v, (x1, x2), 3)
    for i, field in enumerate((w, v)):
        for one in copies[4 + 3 * i : 7 + 3 * i]:
            one.wait()
        pack_rows(pos, field, (y1, y2), 3 * i)


def gather_kernel(slots, slot, order, position, azimuth, incidence, field, *refs):
    *parts, table, out, py1, py2, words = refs
    pos = position()
    planes, blocks = out.shape[1], table.shape[0] - 1
    start = 0
    for step, those in ((1, range(planes)), (2, range(planes)), (0, (-1, planes))):
        entries = [slot(pos, azimuth, incidence, step, x, k) for x in those for k in range(slots)]
        put_slots(words, start, entries, blocks)
        start += words_for(len(entries), blocks)
    per = sum(part.shape[0] for part in parts) // len(order)
    places = [p * per + b for p in order for b in range(per)]
    for part in parts:
        for b in range(part.shape[0]):
            table[places.pop(0)] = part[b].astype(f32) * time_step
    table[table.shape[0] - 1] = jnp.zeros(table.shape[1:], f32)

    def deposit(x, _):
        where = [slot(pos, azimuth, incidence, 0, x, k) for k in range(slots)]
        for c in range(3):
            total = field[c, x]
            for block in where:
                total += table[block, c]
            out[c, x] = total
        return 0

    lax.fori_loop(0, out.shape[1], deposit, 0)
    pack_rows(pos, out, (py1, py2))


def slot_of_table(blocks, per, pos, azimuth, incidence, step, plane, k):
    plane = jnp.clip(pos[2] + plane, 0, incidence.shape[2] - 1)
    block = incidence[azimuth[step], k, plane]
    owner = block // per if per > 1 else block
    slot = (owner ^ pos[3]) * per + block % per if per > 1 else owner ^ pos[3]
    return jnp.where((block >= 0) & (block < blocks), slot, blocks)


def code_of(blocks):
    bits = blocks.bit_length()
    return bits, 24 // bits


def words_for(entries, blocks):
    return -(-entries // code_of(blocks)[1])


def put_slots(ref, start, entries, blocks):
    bits, per = code_of(blocks)
    for i in range(0, len(entries), per):
        word = sum(entry << (bits * j) for j, entry in enumerate(entries[i : i + per]))
        ref[start + i // per] = jnp.full(ref.shape[1:], word.astype(f32))


def slot_reader(ref, start, entries, blocks):
    bits, per = code_of(blocks)
    words = [jnp.max(ref[start + i]).astype(jnp.int32) for i in range(words_for(entries, blocks))]

    def read(entry):
        word = words[0]
        for i, other in enumerate(words[1:], 1):
            word = jnp.where(entry // per == i, other, word)
        return (word >> (entry % per * bits)) & (2**bits - 1)

    return read


def shifted(parts, lane, up):
    out = []
    for i, part in enumerate(parts):
        other = i + 1 if up else i - 1
        edge = pltpu.roll(parts[other], LANES - 1 if up else 1, 1) if 0 <= other < len(parts) else 0.0
        own = pltpu.roll(part, LANES - 1 if up else 1, 1)
        out.append(jnp.where(lane == (LANES - 1 if up else 0), edge, own))
    return out


def local_kernel(step, slots, *refs):
    if step:
        w, v, table, words, grad, out = refs
    else:
        w, v, out, grad = refs
    planes, rows, depth = w.shape[1:]
    slabs = range(depth // LANES)
    chunks = rows // ROWS
    lane = lax.broadcasted_iota(jnp.int32, (ROWS, LANES), 1)
    sub = lax.broadcasted_iota(jnp.int32, (ROWS, LANES), 0)
    comps = range(3)
    if step:
        entries, blocks = planes * slots, table.shape[0] - 1
        read = slot_reader(words, (step - 1) * words_for(entries, blocks), entries, blocks)

    def plane_body(x, _):
        before = jnp.maximum(x - 1, 0)
        after = jnp.minimum(x + 1, planes - 1)
        low = jnp.where(x > 0, slope, 0.0)
        high = jnp.where(x < planes - 1, slope, 0.0)
        deposits = [read(x * slots + k) for k in range(slots)] if step else []

        def place(j, s):
            return slice(j * ROWS, (j + 1) * ROWS), slice(s * LANES, (s + 1) * LANES)

        def load(ref, plane, j):
            return [[ref[(c, plane, *place(j, s))] for s in slabs] for c in comps]

        def along_y(prv, cur, nxt):
            up = pltpu.roll(jnp.where(sub == 0, 0.0 if nxt is None else nxt, cur), ROWS - 1, 0)
            down = pltpu.roll(jnp.where(sub == ROWS - 1, 0.0 if prv is None else prv, cur), 1, 0)
            return up, down

        def pick(window, c, s):
            return [None if a is None else a[c][s] for a in window]

        fld = [None, None, load(w, x, 0)]
        vel = [None, None, load(v, x, 0)]
        for j in range(chunks):
            fld = fld[1:] + [load(w, x, j + 1) if j + 1 < chunks else None]
            vel = vel[1:] + [load(v, x, j + 1) if j + 1 < chunks else None]
            up_z = [shifted(fld[1][c], lane, True) for c in comps]
            down_z = [shifted(fld[1][c], lane, False) for c in comps]
            if not step:
                vel_up_z = [shifted(vel[1][c], lane, True) for c in comps]
                vel_down_z = [shifted(vel[1][c], lane, False) for c in comps]
            for s in slabs:
                v0, v1, v2 = (vel[1][c][s] for c in comps)
                x_up = high - high * v0
                x_down = low + low * v0
                p1, p2 = slope * v1, slope * v2
                y_up, y_down = slope - p1, slope + p1
                z_up, z_down = slope - p2, slope + p2
                w0, w1, w2 = (fld[1][c][s] for c in comps)
                for c in comps:
                    here = place(j, s)
                    if step:
                        g0, g1, g2 = (grad[(3 * i + c, x, *here)] for i in range(3))
                    else:
                        g0 = high * v[(c, after, *here)] - low * v[(c, before, *here)]
                        vuy, vdy = along_y(*pick(vel, c, s))
                        g1 = slope * (vuy - vdy)
                        g2 = slope * (vel_up_z[c][s] - vel_down_z[c][s])
                        terms = [g0, g1, g2]
                        terms[c] += 1.0 - 6.0 * viscous
                        g0, g1, g2 = terms
                        for i, g in enumerate(terms):
                            grad[(3 * i + c, x, *here)] = g
                    wuy, wdy = along_y(*pick(fld, c, s))
                    total = (x_up * w[(c, after, *here)] + x_down * w[(c, before, *here)]) + (y_up * wuy + y_down * wdy)
                    total += (z_up * up_z[c][s] + z_down * down_z[c][s]) + (w0 * g0 + w1 * g1)
                    total += w2 * g2
                    for block in deposits:
                        total += table[(block, c, *here)]
                    out[(c, x, *here)] = total
        return 0

    lax.fori_loop(0, planes, plane_body, 0)


def fix_kernel(step, slots, position, final, *refs):
    pos = position()
    new, *refs = refs
    if step:
        if step == 1:
            table, words, *refs = refs
        v, x1, x2, y1, y2, out, *sends = refs
    else:
        grad, w, v, x1, x2, y1, y2, out, full, *sends = refs
    planes, rows = new.shape[1:3]
    last = planes - 1
    inner = pl.ds(1, planes - 2)
    copies = []
    if step == 1:
        blocks = table.shape[0] - 1
        read = slot_reader(words, 2 * words_for(planes * slots, blocks), 2 * slots, blocks)

    def write(source, target):
        copies.append(pltpu.make_async_copy(source, target, sems.at[len(copies)]))
        copies[-1].start()

    if final:
        result, sems = sends
        middle = pl.ds(ROWS, rows - 2 * ROWS)
        for c in range(3):
            write(out.at[c, inner, middle], result.at[c, inner, middle])

    for low in (True, False):
        row = 0 if low else rows - 1
        there = jnp.where(pos[6 if low else 7] > 0, slope, 0.0)
        sign = there if low else -there
        first = (pos[1] == 0) if not low else (pos[1] != 0)
        coef = there + sign * v[1, :, row, :]
        for c in range(3):
            total = new[c, :, row, :] + coef * jnp.where(first, y1[c], y2[c])
            if not step:
                change = -sign * jnp.where(first, y1[3 + c], y2[3 + c])
                full[3 + c, :, row, :] = grad[3 + c, :, row, :] + change
                total += w[1, :, row, :] * change
            out[c, :, row, :] = total

    if final:
        for c in range(3):
            for tile in (0, rows - ROWS):
                write(out.at[c, inner, pl.ds(tile, ROWS)], result.at[c, inner, pl.ds(tile, ROWS)])

    toward_first = jnp.where(pos[0] == 0, last, 0)
    unscale = 1.0 / field_scales[step]
    for which, halo, plane in ((0, x1, toward_first), (1, x2, last - toward_first)):
        there = jnp.where(pos[4 + which] > 0, slope, 0.0)
        sign = jnp.where(plane > 0, -there, there)
        if step == 1:
            beyond = [read(jnp.where(plane > 0, slots + k, k)) for k in range(slots)]
            coef = there + sign * v[0, plane]
        else:
            coef = (there * unscale) + (sign * unscale) * v[0, plane]
        for c in range(3):
            value = halo[c]
            if step == 1:
                value = value * unscale
                for block in beyond:
                    value += table[block, c]
            total = out[c, plane] + coef * value
            if not step:
                change = (-sign / velocity_scale) * halo[3 + c]
                full[c, plane] = grad[c, plane] + change
                total += w[0, plane] * change
            out[c, plane] = total

    if final:
        for plane in (0, last):
            write(out.at[:, plane], result.at[:, plane])
        for one in copies:
            one.wait()
    else:
        pack_planes(pos, out, sends[:2])
        if step:
            pack_rows(pos, out, sends[2:])


def swaps(axis, wrap):
    count = lax.axis_size(axis)
    pairs = []
    for start in (0, 1):
        both = []
        for i in range(count):
            other = ((i - start) ^ 1) + start
            if not 0 <= other < count:
                other = count - 1 - i if wrap and start and count % 2 == 0 else i
            both.append((i, other))
        pairs.append(both)
    return pairs


def gather_blocks(sources):
    count = lax.axis_size("xz")
    if count & (count - 1):
        return [lax.all_gather(sources, "xz", axis=0, tiled=True)], list(range(count))
    parts, order, stage = [sources], [0], count // 2
    while stage:
        payload = parts[0] if len(parts) == 1 else jnp.concatenate(parts, axis=0)
        parts.append(lax.ppermute(payload, "xz", [(i, i ^ stage) for i in range(count)]))
        order += [p ^ stage for p in order]
        stage //= 2
    return parts, order


def per_device(vorticity, velocity, sources, incidence, azimuth):
    planes, rows, depth = vorticity.shape[1:]
    steps = azimuth.shape[0]
    slots = incidence.shape[2]
    count, side_count = lax.axis_size("xz"), lax.axis_size("gy")
    per = sources.shape[0]
    blocks = count * per

    def position():
        z, y = lax.axis_index("xz"), lax.axis_index("gy")
        even = z % 2 == 0
        low, high = (z > 0).astype(jnp.int32), (z < count - 1).astype(jnp.int32)
        return [
            z % 2,
            y % 2,
            z * planes,
            0 if count & (count - 1) else z,
            jnp.where(even, high, low),
            jnp.where(even, low, high),
            (y > 0).astype(jnp.int32),
            (y < side_count - 1).astype(jnp.int32),
        ]

    incidence = jnp.transpose(incidence, (0, 2, 1))
    x_pairs, y_pairs = swaps("xz", False), swaps("gy", True)
    where = functools.partial(slot_of_table, blocks, per)

    def shape(*dims, dtype=f32):
        return jax.ShapeDtypeStruct(dims, dtype)

    def swap_planes(pair, scale):
        second, first = [lax.ppermute((pair[i] * scale).astype(f16), "xz", x_pairs[i]) for i in (1, 0)]
        return first, second

    def swap_rows(pair):
        return [lax.ppermute(a, "gy", y_pairs[i]) for i, a in enumerate(pair)]

    work = 3 * planes * rows * depth * 40
    whole = shape(3, planes, rows, depth)
    parts, order = gather_blocks(sources)
    vorticity, velocity, *sends = pl.pallas_call(
        functools.partial(load_kernel, position),
        out_shape=[pltpu.VMEM(whole.shape, f32)] * 2
        + [pltpu.VMEM((6, rows, depth), f32)] * 2
        + [pltpu.VMEM((6, planes, depth), f32)] * 2,
        in_specs=[FIXED_HBM, FIXED_HBM],
        out_specs=[VMEM] * 6,
        scratch_shapes=[pltpu.SemaphoreType.DMA((10,))],
        compiler_params=pltpu.CompilerParams(vmem_limit_bytes=VMEM_LIMIT),
    )(in_hbm(vorticity), in_hbm(velocity))
    scale = jnp.array([field_scales[0]] * 3 + [velocity_scale] * 3, f32)[:, None, None]
    halo = swap_planes(sends[:2], scale)
    side = swap_rows(sends[2:])
    field = vorticity
    small = (azimuth, incidence)
    n_words = 2 * words_for(planes * slots, blocks) + words_for(2 * slots, blocks)
    grads = shape(9, planes, rows, depth)
    send_x, send_y = [shape(3, rows, depth)] * 2, [shape(3, planes, depth)] * 2
    for step in range(steps):
        final = step == steps - 1
        local = functools.partial(local_kernel, step, slots)
        fix = functools.partial(fix_kernel, step, slots, position, final)
        if step:
            (new,) = call(local, [whole], field, velocity, table, words, grad, cost=work)
            first = step == 1
            if first:
                one, *side = lax.optimization_barrier((jnp.ones((1, 1, depth), f32), *side))
                halo = [a.astype(f32) * one for a in halo]
            else:
                halo = [a.astype(f32) for a in halo]
            result = call(
                fix,
                [whole, whole] if final else [whole] + send_x + send_y,
                new,
                *([table, words] if first else []),
                velocity,
                *halo,
                *side,
                aliases={0: 0},
                cost=work // 10,
                hbm_out=final,
                scratch=[pltpu.SemaphoreType.DMA((11,))] if final else (),
            )
            if final:
                return result[1]
            field = result[0]
            halo = swap_planes(result[1:3], field_scales[step + 1])
            side = swap_rows(result[3:5])
        else:
            held, parts[1] = lax.optimization_barrier((field, parts[1]))
            new, grad = call(local, [whole, grads], held, velocity, cost=work)
            args = (new, grad, field, velocity, *[a.astype(f32) for a in halo], *side)
            new, grad, *ready = call(fix, [whole, grads] + send_x, *args, aliases={0: 0, 1: 1}, cost=work // 10)
            halo = swap_planes(ready, field_scales[1])
            table, field, *ready, words = call(
                functools.partial(gather_kernel, slots, where, order, position),
                [shape(blocks + 1, 3, rows, depth), whole] + send_y + [shape(n_words, ROWS, LANES)],
                *small,
                new,
                *parts,
                smem=2,
                aliases={2: 1},
                cost=work // 10,
            )
            side = swap_rows(ready)


def solution(mesh):
    in_specs = (
        P(None, ("groups", "xz"), "gy", None),
        P(None, ("groups", "xz"), "gy", None),
        P(("groups", "xz"), None, "gy", None),
        P("groups", None, None),
        P("groups"),
    )
    out_specs = P(None, ("groups", "xz"), "gy", None)
    return jax.shard_map(
        per_device, mesh=mesh, in_specs=in_specs, out_specs=out_specs, check_vma=False
    )
```

```python
import functools

import jax
import jax.numpy as jnp
from jax import lax
from jax.experimental import pallas as pl
from jax.experimental.pallas import tpu as pltpu
from jax.sharding import PartitionSpec as P

time_step = 0.2
viscous = 0.1
slope = 0.5 * time_step

LANES = 128
ROWS = 8
VMEM = pl.BlockSpec(memory_space=pltpu.VMEM)
SMEM = pl.BlockSpec(memory_space=pltpu.SMEM)
HBM = pl.BlockSpec(memory_space=pl.ANY)
FIXED_HBM = pl.BlockSpec(memory_space=pltpu.HBM)
VMEM_LIMIT = 8 * 1024 * 1024
f32 = jnp.float32
f16 = jnp.float16

velocity_scale = 2.0**13
field_scales = (2.0**13, 2.0**10, 2.0**8)


def in_vmem(x):
    return pltpu.with_memory_space_constraint(x, pltpu.VMEM)


def in_hbm(x):
    return pltpu.with_memory_space_constraint(x, pltpu.HBM)


def call(kernel, outs, *args, smem=0, aliases=None, cost=None, hbm_out=False, scratch=()):
    specs = [SMEM] * smem + [VMEM] * (len(args) - smem)
    args = args[:smem] + tuple(in_vmem(a) for a in args[smem:])
    shapes = [pltpu.VMEM(o.shape, o.dtype) for o in outs]
    out_specs = [VMEM] * len(outs)
    if hbm_out:
        shapes[-1], out_specs[-1] = outs[-1], HBM
    return pl.pallas_call(
        kernel,
        out_shape=shapes,
        in_specs=specs,
        out_specs=out_specs,
        scratch_shapes=scratch,
        input_output_aliases=aliases or {},
        compiler_params=pltpu.CompilerParams(vmem_limit_bytes=VMEM_LIMIT),
        cost_estimate=pl.CostEstimate(flops=cost, bytes_accessed=cost // 4, transcendentals=0) if cost else None,
    )(*args)


def pack_planes(pos, field, out_refs, first=0):
    even = pos[0] == 0
    last = field.shape[1] - 1
    toward_first = jnp.where(even, last, 0)
    for out, plane in ((out_refs[0], toward_first), (out_refs[1], last - toward_first)):
        for c in range(3):
            out[first + c] = field[c, plane]


def pack_rows(pos, field, out_refs, first=0):
    even = pos[1] == 0
    for c in range(3):
        low = field[c, :, 0, :]
        high = field[c, :, field.shape[2] - 1, :]
        out_refs[0][first + c] = jnp.where(even, high, low)
        out_refs[1][first + c] = jnp.where(even, low, high)


def load_kernel(position, w_in, v_in, w, v, x1, x2, y1, y2, sems):
    pos = position()
    last = w.shape[1] - 1
    copies = []

    def load(source, target):
        copies.append(pltpu.make_async_copy(source, target, sems.at[len(copies)]))
        copies[-1].start()

    for source, target in ((w_in, w), (v_in, v)):
        for plane in (0, last):
            load(source.at[:, plane], target.at[:, plane])
    inner = pl.ds(1, last - 1)
    for source, target in ((w_in, w), (v_in, v)):
        for c in range(3):
            load(source.at[c, inner], target.at[c, inner])
    for one in copies[:4]:
        one.wait()
    pack_planes(pos, w, (x1, x2), 0)
    pack_planes(pos, v, (x1, x2), 3)
    for i, field in enumerate((w, v)):
        for one in copies[4 + 3 * i : 7 + 3 * i]:
            one.wait()
        pack_rows(pos, field, (y1, y2), 3 * i)


def slots_kernel(slots, slot, planes, blocks, position, azimuth, incidence, *refs):
    *refs, words = refs
    pos = position()
    start = 0
    for step, those in ((0, range(planes)), (1, range(planes)), (2, range(planes)), (0, (-1, planes))):
        entries = [slot(pos, azimuth, incidence, step, x, k) for x in those for k in range(slots)]
        put_slots(words, start, entries, blocks)
        start += words_for(len(entries), blocks)
    local_kernel(0, slots, *refs)


def gather_kernel(slots, order, position, field, words, *refs):
    *parts, table, out, py1, py2 = refs
    pos = position()
    entries, blocks = out.shape[1] * slots, table.shape[0] - 1
    read = slot_reader(words, 0, entries, blocks)
    per = sum(part.shape[0] for part in parts) // len(order)
    places = [p * per + b for p in order for b in range(per)]
    for part in parts:
        for b in range(part.shape[0]):
            table[places.pop(0)] = part[b].astype(f32) * time_step
    table[table.shape[0] - 1] = jnp.zeros(table.shape[1:], f32)

    def deposit(x, _):
        where = [read(x * slots + k) for k in range(slots)]
        for c in range(3):
            total = field[c, x]
            for block in where:
                total += table[block, c]
            out[c, x] = total
        return 0

    lax.fori_loop(0, out.shape[1], deposit, 0)
    pack_rows(pos, out, (py1, py2))


def slot_of_table(blocks, per, pos, azimuth, incidence, step, plane, k):
    plane = jnp.clip(pos[2] + plane, 0, incidence.shape[2] - 1)
    block = incidence[azimuth[step], k, plane]
    owner = block // per if per > 1 else block
    slot = (owner ^ pos[3]) * per + block % per if per > 1 else owner ^ pos[3]
    return jnp.where((block >= 0) & (block < blocks), slot, blocks)


def code_of(blocks):
    bits = blocks.bit_length()
    return bits, 24 // bits


def words_for(entries, blocks):
    return -(-entries // code_of(blocks)[1])


def put_slots(ref, start, entries, blocks):
    bits, per = code_of(blocks)
    for i in range(0, len(entries), per):
        word = sum(entry << (bits * j) for j, entry in enumerate(entries[i : i + per]))
        ref[start + i // per] = jnp.full(ref.shape[1:], word.astype(f32))


def slot_reader(ref, start, entries, blocks):
    bits, per = code_of(blocks)
    words = [jnp.max(ref[start + i]).astype(jnp.int32) for i in range(words_for(entries, blocks))]

    def read(entry):
        word = words[0]
        for i, other in enumerate(words[1:], 1):
            word = jnp.where(entry // per == i, other, word)
        return (word >> (entry % per * bits)) & (2**bits - 1)

    return read


def shifted(parts, lane, up):
    out = []
    for i, part in enumerate(parts):
        other = i + 1 if up else i - 1
        edge = pltpu.roll(parts[other], LANES - 1 if up else 1, 1) if 0 <= other < len(parts) else 0.0
        own = pltpu.roll(part, LANES - 1 if up else 1, 1)
        out.append(jnp.where(lane == (LANES - 1 if up else 0), edge, own))
    return out


def local_kernel(step, slots, *refs):
    if step:
        w, v, table, words, grad, out = refs
    else:
        w, v, out, grad = refs
    planes, rows, depth = w.shape[1:]
    slabs = range(depth // LANES)
    chunks = rows // ROWS
    lane = lax.broadcasted_iota(jnp.int32, (ROWS, LANES), 1)
    sub = lax.broadcasted_iota(jnp.int32, (ROWS, LANES), 0)
    comps = range(3)
    if step:
        entries, blocks = planes * slots, table.shape[0] - 1
        read = slot_reader(words, step * words_for(entries, blocks), entries, blocks)

    def plane_body(x, _):
        before = jnp.maximum(x - 1, 0)
        after = jnp.minimum(x + 1, planes - 1)
        low = jnp.where(x > 0, slope, 0.0)
        high = jnp.where(x < planes - 1, slope, 0.0)
        deposits = [read(x * slots + k) for k in range(slots)] if step else []

        def place(j, s):
            return slice(j * ROWS, (j + 1) * ROWS), slice(s * LANES, (s + 1) * LANES)

        def load(ref, plane, j):
            return [[ref[(c, plane, *place(j, s))] for s in slabs] for c in comps]

        def along_y(prv, cur, nxt):
            up = pltpu.roll(jnp.where(sub == 0, 0.0 if nxt is None else nxt, cur), ROWS - 1, 0)
            down = pltpu.roll(jnp.where(sub == ROWS - 1, 0.0 if prv is None else prv, cur), 1, 0)
            return up, down

        def pick(window, c, s):
            return [None if a is None else a[c][s] for a in window]

        fld = [None, None, load(w, x, 0)]
        vel = [None, None, load(v, x, 0)]
        for j in range(chunks):
            fld = fld[1:] + [load(w, x, j + 1) if j + 1 < chunks else None]
            vel = vel[1:] + [load(v, x, j + 1) if j + 1 < chunks else None]
            up_z = [shifted(fld[1][c], lane, True) for c in comps]
            down_z = [shifted(fld[1][c], lane, False) for c in comps]
            if not step:
                vel_up_z = [shifted(vel[1][c], lane, True) for c in comps]
                vel_down_z = [shifted(vel[1][c], lane, False) for c in comps]
            for s in slabs:
                v0, v1, v2 = (vel[1][c][s] for c in comps)
                x_up = high - high * v0
                x_down = low + low * v0
                p1, p2 = slope * v1, slope * v2
                y_up, y_down = slope - p1, slope + p1
                z_up, z_down = slope - p2, slope + p2
                w0, w1, w2 = (fld[1][c][s] for c in comps)
                for c in comps:
                    here = place(j, s)
                    if step:
                        g0, g1, g2 = (grad[(3 * i + c, x, *here)] for i in range(3))
                    else:
                        g0 = high * v[(c, after, *here)] - low * v[(c, before, *here)]
                        vuy, vdy = along_y(*pick(vel, c, s))
                        g1 = slope * (vuy - vdy)
                        g2 = slope * (vel_up_z[c][s] - vel_down_z[c][s])
                        terms = [g0, g1, g2]
                        terms[c] += 1.0 - 6.0 * viscous
                        g0, g1, g2 = terms
                        for i, g in enumerate(terms):
                            grad[(3 * i + c, x, *here)] = g
                    wuy, wdy = along_y(*pick(fld, c, s))
                    total = (x_up * w[(c, after, *here)] + x_down * w[(c, before, *here)]) + (y_up * wuy + y_down * wdy)
                    total += (z_up * up_z[c][s] + z_down * down_z[c][s]) + (w0 * g0 + w1 * g1)
                    total += w2 * g2
                    for block in deposits:
                        total += table[(block, c, *here)]
                    out[(c, x, *here)] = total
        return 0

    lax.fori_loop(0, planes, plane_body, 0)


def fix_kernel(step, slots, position, final, *refs):
    pos = position()
    new, *refs = refs
    if step:
        if step == 1:
            table, words, *refs = refs
        v, x1, x2, y1, y2, out, *sends = refs
    else:
        grad, w, v, x1, x2, y1, y2, out, full, *sends = refs
    planes, rows = new.shape[1:3]
    last = planes - 1
    inner = pl.ds(1, planes - 2)
    copies = []
    if step == 1:
        blocks = table.shape[0] - 1
        read = slot_reader(words, 3 * words_for(planes * slots, blocks), 2 * slots, blocks)

    def write(source, target):
        copies.append(pltpu.make_async_copy(source, target, sems.at[len(copies)]))
        copies[-1].start()

    if final:
        result, sems = sends
        middle = pl.ds(ROWS, rows - 2 * ROWS)
        for c in range(3):
            write(out.at[c, inner, middle], result.at[c, inner, middle])

    for low in (True, False):
        row = 0 if low else rows - 1
        there = jnp.where(pos[6 if low else 7] > 0, slope, 0.0)
        sign = there if low else -there
        first = (pos[1] == 0) if not low else (pos[1] != 0)
        coef = there + sign * v[1, :, row, :]
        for c in range(3):
            total = new[c, :, row, :] + coef * jnp.where(first, y1[c], y2[c])
            if not step:
                change = -sign * jnp.where(first, y1[3 + c], y2[3 + c])
                full[3 + c, :, row, :] = grad[3 + c, :, row, :] + change
                total += w[1, :, row, :] * change
            out[c, :, row, :] = total

    if final:
        for c in range(3):
            for tile in (0, rows - ROWS):
                write(out.at[c, inner, pl.ds(tile, ROWS)], result.at[c, inner, pl.ds(tile, ROWS)])

    toward_first = jnp.where(pos[0] == 0, last, 0)
    unscale = 1.0 / field_scales[step]
    for which, halo, plane in ((0, x1, toward_first), (1, x2, last - toward_first)):
        there = jnp.where(pos[4 + which] > 0, slope, 0.0)
        sign = jnp.where(plane > 0, -there, there)
        if step == 1:
            beyond = [read(jnp.where(plane > 0, slots + k, k)) for k in range(slots)]
            coef = there + sign * v[0, plane]
        else:
            coef = (there * unscale) + (sign * unscale) * v[0, plane]
        for c in range(3):
            value = halo[c]
            if step == 1:
                value = value * unscale
                for block in beyond:
                    value += table[block, c]
            total = out[c, plane] + coef * value
            if not step:
                change = (-sign / velocity_scale) * halo[3 + c]
                full[c, plane] = grad[c, plane] + change
                total += w[0, plane] * change
            out[c, plane] = total

    if final:
        for plane in (0, last):
            write(out.at[:, plane], result.at[:, plane])
        for one in copies:
            one.wait()
    else:
        pack_planes(pos, out, sends[:2])
        if step:
            pack_rows(pos, out, sends[2:])


def swaps(axis, wrap):
    count = lax.axis_size(axis)
    pairs = []
    for start in (0, 1):
        both = []
        for i in range(count):
            other = ((i - start) ^ 1) + start
            if not 0 <= other < count:
                other = count - 1 - i if wrap and start and count % 2 == 0 else i
            both.append((i, other))
        pairs.append(both)
    return pairs


def gather_blocks(sources):
    count = lax.axis_size("xz")
    if count & (count - 1):
        return [lax.all_gather(sources, "xz", axis=0, tiled=True)], list(range(count))
    parts, order, stage = [sources], [0], count // 2
    while stage:
        payload = parts[0] if len(parts) == 1 else jnp.concatenate(parts, axis=0)
        parts.append(lax.ppermute(payload, "xz", [(i, i ^ stage) for i in range(count)]))
        order += [p ^ stage for p in order]
        stage //= 2
    return parts, order


def per_device(vorticity, velocity, sources, incidence, azimuth):
    planes, rows, depth = vorticity.shape[1:]
    steps = azimuth.shape[0]
    slots = incidence.shape[2]
    count, side_count = lax.axis_size("xz"), lax.axis_size("gy")
    per = sources.shape[0]
    blocks = count * per

    def position():
        z, y = lax.axis_index("xz"), lax.axis_index("gy")
        even = z % 2 == 0
        low, high = (z > 0).astype(jnp.int32), (z < count - 1).astype(jnp.int32)
        return [
            z % 2,
            y % 2,
            z * planes,
            0 if count & (count - 1) else z,
            jnp.where(even, high, low),
            jnp.where(even, low, high),
            (y > 0).astype(jnp.int32),
            (y < side_count - 1).astype(jnp.int32),
        ]

    incidence = jnp.transpose(incidence, (0, 2, 1))
    x_pairs, y_pairs = swaps("xz", False), swaps("gy", True)
    where = functools.partial(slot_of_table, blocks, per)

    def shape(*dims, dtype=f32):
        return jax.ShapeDtypeStruct(dims, dtype)

    def swap_planes(pair, scale):
        second, first = [lax.ppermute((pair[i] * scale).astype(f16), "xz", x_pairs[i]) for i in (1, 0)]
        return first, second

    def swap_rows(pair):
        return [lax.ppermute(a, "gy", y_pairs[i]) for i, a in enumerate(pair)]

    work = 3 * planes * rows * depth * 40
    whole = shape(3, planes, rows, depth)
    parts, order = gather_blocks(sources)
    vorticity, velocity, *sends = pl.pallas_call(
        functools.partial(load_kernel, position),
        out_shape=[pltpu.VMEM(whole.shape, f32)] * 2
        + [pltpu.VMEM((6, rows, depth), f32)] * 2
        + [pltpu.VMEM((6, planes, depth), f32)] * 2,
        in_specs=[FIXED_HBM, FIXED_HBM],
        out_specs=[VMEM] * 6,
        scratch_shapes=[pltpu.SemaphoreType.DMA((10,))],
        compiler_params=pltpu.CompilerParams(vmem_limit_bytes=VMEM_LIMIT),
    )(in_hbm(vorticity), in_hbm(velocity))
    scale = jnp.array([field_scales[0]] * 3 + [velocity_scale] * 3, f32)[:, None, None]
    halo = swap_planes(sends[:2], scale)
    side = swap_rows(sends[2:])
    field = vorticity
    n_words = 3 * words_for(planes * slots, blocks) + words_for(2 * slots, blocks)
    grads = shape(9, planes, rows, depth)
    send_x, send_y = [shape(3, rows, depth)] * 2, [shape(3, planes, depth)] * 2
    for step in range(steps):
        final = step == steps - 1
        local = functools.partial(local_kernel, step, slots)
        fix = functools.partial(fix_kernel, step, slots, position, final)
        if step:
            (new,) = call(local, [whole], field, velocity, table, words, grad, cost=work)
            first = step == 1
            if first:
                one, *side = lax.optimization_barrier((jnp.ones((1, 1, depth), f32), *side))
                halo = [a.astype(f32) * one for a in halo]
            else:
                halo = [a.astype(f32) for a in halo]
            result = call(
                fix,
                [whole, whole] if final else [whole] + send_x + send_y,
                new,
                *([table, words] if first else []),
                velocity,
                *halo,
                *side,
                aliases={0: 0},
                cost=work // 10,
                hbm_out=final,
                scratch=[pltpu.SemaphoreType.DMA((11,))] if final else (),
            )
            if final:
                return result[1]
            field = result[0]
            halo = swap_planes(result[1:3], field_scales[step + 1])
            side = swap_rows(result[3:5])
        else:
            held, parts[1] = lax.optimization_barrier((field, parts[1]))
            new, grad, words = call(
                functools.partial(slots_kernel, slots, where, planes, blocks, position),
                [whole, grads, shape(n_words, ROWS, LANES)],
                azimuth,
                incidence,
                held,
                velocity,
                smem=2,
                cost=work,
            )
            args = (new, grad, field, velocity, *[a.astype(f32) for a in halo], *side)
            new, grad, *ready = call(fix, [whole, grads] + send_x, *args, aliases={0: 0, 1: 1}, cost=work // 10)
            halo = swap_planes(ready, field_scales[1])
            table, field, *ready = call(
                functools.partial(gather_kernel, slots, order, position),
                [shape(blocks + 1, 3, rows, depth), whole] + send_y,
                new,
                words,
                *parts,
                aliases={0: 1},
                cost=work // 10,
            )
            side = swap_rows(ready)


def solution(mesh):
    in_specs = (
        P(None, ("groups", "xz"), "gy", None),
        P(None, ("groups", "xz"), "gy", None),
        P(("groups", "xz"), None, "gy", None),
        P("groups", None, None),
        P("groups"),
    )
    out_specs = P(None, ("groups", "xz"), "gy", None)
    return jax.shard_map(
        per_device, mesh=mesh, in_specs=in_specs, out_specs=out_specs, check_vma=False
    )
```
